512 devices in a mesh: panel: 128 (over y, z, core), obs: 4 (over x).
Axes of the slice: x: 4, y: 4, z: 16, core: 2. Of those that a mesh axis runs over, the one named last changes fastest.
Arguments:
- surface: float32 [4, 8, 2, 131072], P(None, None, None, 'panel'), may hold values from -6 to 6
- fluid_owner: int32 [32768, 1], P('panel'), may hold values from 0 to 127; in each aligned block of 256 rows (0 to 255, 256 to 511, ...) at most 8 rows name the same one
- cell_row: int32 [32768], P('panel'), may hold values from 0 to 1023
- pan_polar: float32 [32768], P('panel'), may hold values from 0 to 3.14159
- pan_azimuth: float32 [32768], P('panel'), may hold values from -3.140625 to 3.140625
- pan_radius: float32 [32768], P('panel'), may hold values from 0.8 to 1.2
- pan_area: float32 [32768], P('panel'), may hold values from 0.5 to 2
- obs_polar: float32 [16384], P(('panel', 'obs')), may hold values from 0 to 3.14159
- obs_azimuth: float32 [16384], P(('panel', 'obs')), may hold values from -3.140625 to 3.140625
- obs_distance: float32 [16384], P(('panel', 'obs')), may hold values from 5 to 20
- harmonic: int32 [2], replicated, may hold values from 1 to 8, as said below
Outputs:
- spectrum: float32 [2, 2, 16384], P(None, None, ('panel', 'obs'))
The draws below stay inside these ranges and needn't reach their ends.
Inputs may be any that keep to these rules, and one draw needn't show every extreme that they name: `fluid_owner`: within the rows of one device (aligned blocks of 256 panels) no fluid owner is named by more than 8 panels, a bound that some block reaches. The 2 harmonic numbers differ, and one of them is 8.
All inputs are finite; a program needn't handle non-finite values.
Results may differ from the reference program's by a relative error of at most 0.0003.
Values sent between devices are 32-bit elements; how exact they have to be, the bound alone decides.
No kernel may reach another device: no remote copies, remote signals or barrier semaphores. Data moves between devices by JAX's collectives and lax.ppermute only.
A program may use at most 64 MiB of HBM per device.

```python
import math
import jax
import jax.numpy as jnp
import numpy as np
from jax import lax

VARS = 4
HARM = 8
PICK = 2
PAN_DEV = 256
CELL_DEV = 1024
CAP = 8
PANELS = 32768
CELLS = 131072
OBS = 16384
N_PANEL = 128


def draw_harmonic(key, part):
    key = jax.random.fold_in(key, 11)
    other_key, order_key = jax.random.split(key)
    other = jax.random.randint(other_key, (), 1, HARM)
    flip = jax.random.randint(order_key, (), 0, 2)
    top = jnp.full((), HARM, jnp.int32)
    first = jnp.where(flip == 0, top, other)
    second = jnp.where(flip == 0, other, top)
    pair = jnp.stack([first, second]).astype(jnp.int32)
    rest = jnp.zeros((PICK - 2,), jnp.int32) + pair[1]
    return jnp.concatenate([pair, rest])[:PICK].astype(jnp.int32)


def plant(values, stream_key, smallest, high):
    longest = values.shape.index(max(values.shape))
    spots = []
    for shift in (0, 1):
        where = [jax.random.randint(jax.random.fold_in(stream_key, axis), (), 0, length) for axis, length in enumerate(values.shape)]
        where[longest] = (where[longest] + shift) % values.shape[longest]
        spots.append(tuple(where))
    return values.at[spots[0]].set(smallest).at[spots[1]].set(high)


def level_of(stream_key, shape, shards, low, top_value):
    def one(position, blocks):
        steps = jax.random.uniform(jax.random.fold_in(jax.random.fold_in(stream_key, 6), position), (blocks,), jnp.float32, low / len(shards), top_value / len(shards))
        return jnp.repeat(jnp.exp(steps), shape[position] // blocks).reshape((-1,) + (1,) * (len(shape) - position - 1))

    gain = one(*shards[0])
    for cut in shards[1:]:
        gain = gain * one(*cut)
    return gain


def assign_block(rng, own, number, rows, number_of, top, bound, slope):
    order = jax.random.permutation(rng, number_of)
    packed, usual = portions_of(number_of, rows * top, bound, slope, True), portions_of(number_of, rows * top, bound, slope, False)
    places = jnp.arange(number_of)

    def named(sizes, turn):
        used = int((sizes > 0).sum())
        fixed = max(1, used // 4)
        shifted = fixed + (places - fixed + turn * (used - fixed)) % max(1, number_of - fixed)
        return jnp.zeros((number_of,), jnp.int32).at[order[jnp.where(places < fixed, places, shifted)]].set(jnp.asarray(sizes, jnp.int32))

    sizes = jnp.where(number % 4 == 0, named(packed, number // 4), named(usual, number - number // 4 - 1))
    mixed = jax.random.permutation(jax.random.fold_in(own, 3), number_of)
    giver, receiver = mixed[0:number_of // 2 * 2:2], mixed[1:number_of // 2 * 2:2]
    slack = jnp.minimum(sizes[giver] - 1, bound - sizes[receiver]) // 2
    slack = jnp.where((giver == order[0]) | (receiver == order[0]) | (sizes[receiver] == 0), 0, jnp.maximum(slack, 0))
    shifted = jax.random.randint(jax.random.fold_in(own, 4), (number_of // 2,), 0, 1 << 20) % (slack + 1)
    sizes = sizes.at[giver].add(-shifted).at[receiver].add(shifted)
    members = jnp.searchsorted(jnp.cumsum(sizes), jnp.arange(rows * top), side="right").astype(jnp.int32)
    table = members.reshape(top, rows).T
    table = table[jax.random.permutation(jax.random.fold_in(own, 1), rows)]
    turn = jax.random.randint(jax.random.fold_in(own, 2), (rows, 1), 0, top)
    return jnp.take_along_axis(table, (jnp.arange(top)[None, :] + turn) % top, axis=1)


def portions_of(number_of, total, bound, lean, full):
    loads = [(1 << 20) // math.isqrt(standing ** lean) + 1 for standing in range(1, number_of + 1)]
    largest = bound if full else min(bound, max(-(-total // number_of), total * loads[0] // sum(loads)))
    least = 1 if total - largest >= number_of - 1 else 0
    given, surplus = [largest] + [least] * (number_of - 1), total - largest - least * (number_of - 1)
    while surplus > 0:
        free = [i for i in range(1, number_of) if given[i] < largest] or [i for i in range(1, number_of) if given[i] < bound]
        mass, left = sum([loads[i] for i in free]), surplus
        for i in free:
            more = min(bound - given[i], max(1, left * loads[i] // mass), surplus)
            given[i] = given[i] + more
            surplus = surplus - more
    return np.array(given)


def gaussian(rng, dims, deviation, most, cuts=(), dtype=jnp.bfloat16):
    values = deviation * jax.random.normal(rng, dims, jnp.float32)
    if cuts:
        values = values * level_of(rng, dims, cuts, -0.22, 0.18)
    return jnp.clip(values, -most, most).astype(dtype)


def setup_inputs(seed: int = 0) -> dict:
    keys = jax.random.split(jax.random.key(seed), 12)
    surface = gaussian(keys[0], (VARS, HARM, 2, CELLS), 1.0, 6.0, ((3, 128),), jnp.float32)
    fluid_owner_keys = jax.random.split(jax.random.fold_in(keys[1], 1), PANELS // PAN_DEV)
    fluid_owner_turns = jax.random.permutation(jax.random.fold_in(keys[1], 3), PANELS // PAN_DEV)
    fluid_owner = jax.vmap(lambda own, number: assign_block(jax.random.fold_in(keys[1], 2), own, number, PAN_DEV, N_PANEL, 1, CAP, 2))(fluid_owner_keys, fluid_owner_turns).reshape((PANELS, 1))
    cell_row = plant(jax.random.randint(keys[2], (PANELS,), 0, CELL_DEV), jax.random.fold_in(keys[2], 1), 0, CELL_DEV - 1).astype(jnp.int32)
    pan_polar = jnp.clip(3.14159 * jax.random.uniform(keys[3], (PANELS,), jnp.float32) ** level_of(keys[3], (PANELS,), ((0, 128),), -0.2, 0.2), 0.0, 3.14159)
    pan_azimuth = jnp.clip(jax.random.uniform(keys[4], (PANELS,), jnp.float32, -3.140625, 3.140625), -3.140625, 3.140625)
    pan_radius = jnp.clip(0.8 + 0.40000004 * jax.random.uniform(keys[5], (PANELS,), jnp.float32) ** level_of(keys[5], (PANELS,), ((0, 128),), -0.2, 0.2), 0.8, 1.2)
    pan_area = jnp.clip(0.5 + 1.5 * jax.random.uniform(keys[6], (PANELS,), jnp.float32) ** level_of(keys[6], (PANELS,), ((0, 128),), -0.2, 0.2), 0.5, 2.0)
    obs_polar = jnp.clip(3.14159 * jax.random.uniform(keys[7], (OBS,), jnp.float32) ** level_of(keys[7], (OBS,), ((0, 512),), -0.2, 0.2), 0.0, 3.14159)
    obs_azimuth = jnp.clip(jax.random.uniform(keys[8], (OBS,), jnp.float32, -3.140625, 3.140625), -3.140625, 3.140625)
    obs_distance = jnp.clip(jnp.exp(math.log(20.0) - 1.3862944 * jax.random.uniform(keys[9], (OBS,), jnp.float32) ** level_of(keys[9], (OBS,), ((0, 512),), -0.2, 0.2)), 5.0, 20.0)
    harmonic = draw_harmonic(jax.random.fold_in(keys[11], 71), 0)
    return {"surface": surface, "fluid_owner": fluid_owner, "cell_row": cell_row, "pan_polar": pan_polar, "pan_azimuth": pan_azimuth, "pan_radius": pan_radius, "pan_area": pan_area, "obs_polar": obs_polar, "obs_azimuth": obs_azimuth, "obs_distance": obs_distance, "harmonic": harmonic}


BASE_WAVE = 2.0

def directions(polar, azimuth):
    cycle = jnp.sin(polar)
    return jnp.stack([cycle * jnp.cos(azimuth), cycle * jnp.sin(azimuth), jnp.cos(polar)])

def sources(picked, normal, pan_area, panel_total):
    weight = pan_area * (1.0 / math.sqrt(panel_total))
    flux_real = (picked[1, :, 0] * normal[0] + picked[2, :, 0] * normal[1] + picked[3, :, 0] * normal[2]) * weight
    flux_imag = (picked[1, :, 1] * normal[0] + picked[2, :, 1] * normal[1] + picked[3, :, 1] * normal[2]) * weight
    press_real = picked[0, :, 0] * weight
    press_imag = picked[0, :, 1] * weight
    return (flux_real, flux_imag, press_real, press_imag)

def tile_sum(observer, panel_pos, normal, terms, waves):
    flux_real, flux_imag, press_real, press_imag = terms
    delta_x = observer[0][:, None] - panel_pos[0][None, :]
    delta_y = observer[1][:, None] - panel_pos[1][None, :]
    delta_z = observer[2][:, None] - panel_pos[2][None, :]
    distance = jnp.sqrt(delta_x * delta_x + delta_y * delta_y + delta_z * delta_z)
    inverse = 1.0 / distance
    cosine = (delta_x * normal[0][None, :] + delta_y * normal[1][None, :] + delta_z * normal[2][None, :]) * inverse
    green_factor = inverse * (0.25 / math.pi)
    parts = []
    for which in range(waves.shape[0]):
        wave = waves[which]
        phase = wave * distance
        cos_phase = jnp.cos(phase)
        sin_phase = jnp.sin(phase)
        dip_real = press_real[which][None, :] * cosine
        dip_imag = press_imag[which][None, :] * cosine
        mix_real = -wave * flux_imag[which][None, :] + dip_real * inverse - wave * dip_imag
        mix_imag = wave * flux_real[which][None, :] + dip_imag * inverse + wave * dip_real
        parts.append(lax.optimization_barrier(jnp.sum(green_factor * (cos_phase * mix_real + sin_phase * mix_imag), axis=1)))
        parts.append(lax.optimization_barrier(jnp.sum(green_factor * (cos_phase * mix_imag - sin_phase * mix_real), axis=1)))
    return jnp.stack(parts).reshape(waves.shape[0], 2, observer.shape[1])

def reference(surface, fluid_owner, cell_row, pan_polar, pan_azimuth, pan_radius, pan_area, obs_polar, obs_azimuth, obs_distance, harmonic):
    cell_index = (fluid_owner[:, 0] * CELL_DEV + cell_row).astype(jnp.int32)
    rows = jnp.take(surface, cell_index, axis=3)
    picked = jnp.take(rows, (harmonic - 1).astype(jnp.int32), axis=1)
    normal = directions(pan_polar, pan_azimuth)
    panel_pos = normal * pan_radius[None, :]
    terms = sources(picked, normal, pan_area, PANELS)
    waves = BASE_WAVE * harmonic.astype(jnp.float32)
    observer = directions(obs_polar, obs_azimuth) * obs_distance[None, :]
    block_size = 128 if OBS % 128 == 0 else OBS
    blocks = observer.reshape(3, OBS // block_size, block_size).transpose(1, 0, 2)

    def one_block(piece):
        return tile_sum(piece, panel_pos, normal, terms, waves)
    spectra = lax.map(one_block, blocks)
    spectra = spectra.transpose(1, 2, 0, 3).reshape(PICK, 2, OBS)
    return spectra * obs_distance[None, None, :]
```

```python
import functools
import math

import jax
import jax.numpy as jnp
from jax import lax
from jax.experimental import pallas as pl
from jax.experimental.pallas import tpu as pltpu
from jax.sharding import PartitionSpec as P

BASE_WAVE = 2.0
LANES = 128
SLOTS = 8
MAGIC = 12582912.0
F32 = jnp.float32
BF16 = jnp.bfloat16
VMEM_LIMIT = 48 * 1024 * 1024

SIN_HALF = (6.283164024353027, -10.334285736083984, 5.083797931671143, -1.1092723608016968)
COS_HALF = (1.9999998807907104, -9.869585990905762, 8.11682415008545, -2.6637604236602783, 0.4393935799598694)


def split3(value):
    high = value.astype(BF16).astype(F32)
    rest = value - high
    mid = rest.astype(BF16).astype(F32)
    return high, mid, rest - mid


def owner_mask(owner):
    rows = lax.broadcasted_iota(jnp.int32, (LANES, owner.shape[1]), 0)
    return jnp.where(rows == owner, 1.0, 0.0).astype(F32)


def rank_of(member):
    count = member.shape[1]
    first = lax.broadcasted_iota(jnp.int32, (count, count), 0)
    second = lax.broadcasted_iota(jnp.int32, (count, count), 1)
    earlier = jnp.where(first < second, 1.0, 0.0).astype(BF16)
    before = jnp.dot(member.astype(BF16), earlier, preferred_element_type=F32)
    return jnp.sum(before * member, axis=0, keepdims=True)


def ask_kernel(owner_ref, cell_ref, polar_ref, azimuth_ref, distance_ref, out_ref):
    member = owner_mask(owner_ref[...])
    rank = rank_of(member)
    cell = cell_ref[...]
    low = (cell & 31).astype(F32)
    high = (cell >> 5).astype(F32)
    slot = lax.broadcasted_iota(jnp.int32, (LANES, cell.shape[1]), 0)
    here = jnp.where((slot & 7).astype(F32) == rank, 1.0, 0.0)
    table = here * jnp.where(slot < 8, low, jnp.where(slot < 16, high, 0.0))
    asked = lax.dot_general(
        member.astype(BF16),
        table.astype(BF16),
        (((1,), (1,)), ((), ())),
        preferred_element_type=F32,
    )
    asked = asked + 32.0 * pltpu.roll(asked, LANES - 8, 1)
    lane = lax.broadcasted_iota(jnp.int32, (LANES, LANES), 1)
    polar = polar_ref[...]
    azimuth = azimuth_ref[...]
    distance = distance_ref[...]
    cycle = jnp.sin(polar) * distance
    place = jnp.concatenate(
        [
            jnp.zeros_like(polar),
            cycle * jnp.cos(azimuth),
            cycle * jnp.sin(azimuth),
            distance * jnp.cos(polar),
        ],
        axis=1,
    )
    out_ref[...] = jnp.where(lane < 8, asked, jnp.broadcast_to(place, (LANES, LANES)))


def pick_kernel(harmonic_ref, ask_ref, surface_ref, out_ref, rows_ref):
    wanted = jnp.transpose(ask_ref[...])[0:SLOTS].astype(jnp.int32)
    block = wanted >> 7
    within = wanted & 127
    chunks = surface_ref.shape[3] // LANES
    values = []
    for var in range(4):
        for which in range(2):
            values.append(surface_ref[var, harmonic_ref[which] - 1])
    values = jnp.concatenate(values, axis=0)
    for slot in range(SLOTS):
        index = jnp.broadcast_to(within[slot : slot + 1], (16, LANES))
        where = jnp.broadcast_to(block[slot : slot + 1], (16, LANES))
        found = jnp.zeros((16, LANES), F32)
        for chunk in range(chunks):
            part = values[:, chunk * LANES : (chunk + 1) * LANES]
            taken = jnp.take_along_axis(part, index, axis=1)
            found = jnp.where(where == chunk, taken, found)
        rows_ref[slot * 16 : slot * 16 + 16, :] = found
    out_ref[...] = jnp.transpose(rows_ref[...])


def radiate_kernel(
    harmonic_ref,
    ask_ref,
    answer_ref,
    owner_ref,
    polar_ref,
    azimuth_ref,
    radius_ref,
    area_ref,
    out_ref,
    panel_ref,
    observer_ref,
    linear_ref,
    rows_ref,
    *,
    panel_total,
):
    count = owner_ref.shape[1]
    member = owner_mask(owner_ref[...])
    rank = rank_of(member)
    spread = jnp.zeros((LANES, count), F32)
    for part in split3(answer_ref[...]):
        spread = spread + lax.dot_general(
            part.astype(BF16),
            member.astype(BF16),
            (((0,), (0,)), ((), ())),
            preferred_element_type=F32,
        )
    picked = jnp.zeros((16, count), F32)
    for slot in range(SLOTS):
        picked = picked + jnp.where(rank == slot, spread[slot * 16 : slot * 16 + 16], 0.0)

    polar = polar_ref[...]
    azimuth = azimuth_ref[...]
    radius = radius_ref[...]
    cycle = jnp.sin(polar)
    normal = (cycle * jnp.cos(azimuth), cycle * jnp.sin(azimuth), jnp.cos(polar))
    weight = area_ref[...] * (0.125 / (math.pi * math.sqrt(panel_total)))

    def row(var, which, part):
        at = var * 4 + which * 2 + part
        return picked[at : at + 1] * weight

    line = lax.broadcasted_iota(jnp.int32, (8, count), 0)

    def stack(*rows):
        total = jnp.zeros((8, count), F32)
        for at, value in enumerate(rows):
            total = jnp.where(line == at, value, total)
        return total

    square = stack(
        jnp.ones_like(radius),
        radius * radius,
        *[-2.0 * radius * axis for axis in normal],
    )
    offset = stack(jnp.zeros_like(radius), -radius, *normal)
    quantities = [square]
    for which in range(2):
        wave = BASE_WAVE * harmonic_ref[which].astype(F32)
        flux = [
            wave
            * (
                row(1, which, part) * normal[0]
                + row(2, which, part) * normal[1]
                + row(3, which, part) * normal[2]
            )
            for part in range(2)
        ]
        press = [row(0, which, part) for part in range(2)]
        quantities.append(square * (-flux[1]) + offset * press[0])
        quantities.append(square * flux[0] + offset * press[1])
        quantities.append(offset * (wave * press[0]))
        quantities.append(offset * (wave * press[1]))
    for number, quantity in enumerate(quantities):
        high, mid, low = split3(quantity)
        zero = jnp.zeros((80, count), F32)
        tall = jnp.concatenate([high, mid, low, high, mid, high, zero], axis=0)
        for half in range(count // LANES):
            panel_ref[pl.ds(number * count + half * LANES, LANES), :] = jnp.transpose(
                tall[:, half * LANES : (half + 1) * LANES]
            ).astype(BF16)

    place = jnp.transpose(ask_ref[...])
    few = lax.broadcasted_iota(jnp.int32, (8, LANES), 0)
    for number in range(32):
        axes = [place[32 * axis + number : 32 * axis + number + 1] for axis in (1, 2, 3)]
        dist = axes[0] * axes[0] + axes[1] * axes[1] + axes[2] * axes[2]
        total = jnp.where(few == 0, dist, jnp.where(few == 1, 1.0, 0.0))
        for at, value in enumerate(axes):
            total = jnp.where(few == at + 2, value, total)
        high, mid, low = split3(total)
        zero = jnp.zeros((80, LANES), F32)
        tall = jnp.concatenate([high, high, high, mid, mid, low, zero], axis=0)
        observer_ref[number // 2, :, (number % 2) * LANES : (number % 2 + 1) * LANES] = tall.astype(BF16)

    turns = [harmonic_ref[which].astype(F32) * (BASE_WAVE / (2.0 * math.pi)) for which in range(2)]

    def one_tile(tile, carry):
        linear_ref[...] = jnp.dot(panel_ref[...], observer_ref[tile], preferred_element_type=F32)
        for side in range(2):
            lanes = pl.ds(side * LANES, LANES)

            def group(step, sums):
                sums = list(sums)
                for sub in range(4):
                    base = pl.multiple_of(step * 32, 32) + sub * 8

                    def get(number):
                        return linear_ref[pl.ds(base + number * count, 8), lanes]

                    far = get(0)
                    inverse = lax.rsqrt(far)
                    distance = far * inverse
                    cube = inverse * inverse * inverse
                    for which in range(2):
                        phase = distance * turns[which]
                        phase = phase - ((phase + MAGIC) - MAGIC)
                        z = phase * phase
                        sine = SIN_HALF[-1]
                        for coef in SIN_HALF[-2::-1]:
                            sine = sine * z + coef
                        sine = sine * phase
                        cosine = COS_HALF[-1]
                        for coef in COS_HALF[-2::-1]:
                            cosine = cosine * z + coef
                        sine = sine * cosine
                        cosine = cosine * cosine - 2.0
                        sine = sine * cube
                        cosine = cosine * cube
                        real = get(1 + 4 * which) - distance * get(4 + 4 * which)
                        imag = get(2 + 4 * which) + distance * get(3 + 4 * which)
                        sums[2 * which] = sums[2 * which] + (cosine * real + sine * imag)
                        sums[2 * which + 1] = sums[2 * which + 1] + (cosine * imag - sine * real)
                return tuple(sums)

            zero = jnp.zeros((8, LANES), F32)
            sums = lax.fori_loop(0, count // 32, group, (zero,) * 4)
            for at in range(4):
                rows_ref[pl.ds(at * 32 + tile * 2 + side, 1), :] = jnp.sum(sums[at], axis=0, keepdims=True)
        return carry

    lax.fori_loop(0, 16, one_tile, 0)
    out_ref[...] = jnp.transpose(rows_ref[...])


def vmem():
    return pl.BlockSpec(memory_space=pltpu.VMEM)


def smem():
    return pl.BlockSpec(memory_space=pltpu.SMEM)


def exchange(value):
    return lax.all_to_all(value, "panel", split_axis=0, concat_axis=0, tiled=True)


def local(
    surface,
    fluid_owner,
    cell_row,
    pan_polar,
    pan_azimuth,
    pan_radius,
    pan_area,
    obs_polar,
    obs_azimuth,
    obs_distance,
    harmonic,
):
    per_device = cell_row.shape[0]
    panel_total = per_device * lax.axis_size("panel")
    owner = fluid_owner.reshape(1, per_device)
    table = jax.ShapeDtypeStruct((LANES, LANES), F32)
    params = pltpu.CompilerParams(vmem_limit_bytes=VMEM_LIMIT)
    ask = pl.pallas_call(
        ask_kernel,
        out_shape=table,
        in_specs=[vmem()] * 5,
        out_specs=vmem(),
        compiler_params=params,
        name="ask",
    )(
        owner,
        cell_row.reshape(1, per_device),
        obs_polar.reshape(1, -1),
        obs_azimuth.reshape(1, -1),
        obs_distance.reshape(1, -1),
    )
    ask = exchange(ask)
    answer = pl.pallas_call(
        pick_kernel,
        out_shape=table,
        in_specs=[smem(), vmem(), vmem()],
        out_specs=vmem(),
        scratch_shapes=[pltpu.VMEM((LANES, LANES), F32)],
        compiler_params=params,
        name="pick",
    )(harmonic, ask, surface)
    answer = exchange(answer)
    partial = pl.pallas_call(
        functools.partial(radiate_kernel, panel_total=panel_total),
        out_shape=table,
        in_specs=[smem()] + [vmem()] * 7,
        out_specs=vmem(),
        scratch_shapes=[
            pltpu.VMEM((9 * per_device, LANES), BF16),
            pltpu.VMEM((16, LANES, 2 * LANES), BF16),
            pltpu.VMEM((9 * per_device, 2 * LANES), F32),
            pltpu.VMEM((LANES, LANES), F32),
        ],
        compiler_params=params,
        name="radiate",
    )(
        harmonic,
        ask,
        answer,
        owner,
        pan_polar.reshape(1, -1),
        pan_azimuth.reshape(1, -1),
        pan_radius.reshape(1, -1),
        pan_area.reshape(1, -1),
    )
    partial = exchange(partial)
    summed = jnp.sum(partial, axis=0).reshape(2, 2, obs_distance.shape[0])
    return summed * obs_distance[None, None, :]


def solution(mesh):
    in_specs = (
        P(None, None, None, "panel"),
        P("panel", None),
        P("panel"),
        P("panel"),
        P("panel"),
        P("panel"),
        P("panel"),
        P(("panel", "obs")),
        P(("panel", "obs")),
        P(("panel", "obs")),
        P(),
    )
    out_specs = P(None, None, ("panel", "obs"))
    return jax.shard_map(local, mesh=mesh, in_specs=in_specs, out_specs=out_specs, check_vma=False)
```

```python
import functools
import math

import jax
import jax.numpy as jnp
from jax import lax
from jax.experimental import pallas as pl
from jax.experimental.pallas import tpu as pltpu
from jax.sharding import PartitionSpec as P

BASE_WAVE = 2.0
LANES = 128
SLOTS = 8
MAGIC = 12582912.0
F32 = jnp.float32
BF16 = jnp.bfloat16
VMEM_LIMIT = 48 * 1024 * 1024
TILES = 16

TAN_TOP = (3.1051745414733887, -2.988323211669922)
TAN_LOW = (0.9884211421012878, -4.203673839569092)


def split3(value):
    high = value.astype(BF16).astype(F32)
    rest = value - high
    mid = rest.astype(BF16).astype(F32)
    return high, mid, rest - mid


def owner_mask(owner):
    rows = lax.broadcasted_iota(jnp.int32, (LANES, owner.shape[1]), 0)
    return jnp.where(rows == owner, 1.0, 0.0).astype(F32)


def rank_of(member):
    count = member.shape[1]
    first = lax.broadcasted_iota(jnp.int32, (count, count), 0)
    second = lax.broadcasted_iota(jnp.int32, (count, count), 1)
    earlier = jnp.where(first < second, 1.0, 0.0).astype(BF16)
    before = jnp.dot(member.astype(BF16), earlier, preferred_element_type=F32)
    return jnp.sum(before * member, axis=0, keepdims=True)


def fetch(sources, targets, sem):
    copies = [pltpu.make_async_copy(*pair, sem.at[at]) for at, pair in enumerate(zip(sources, targets))]
    for copy in copies:
        copy.start()
    for copy in copies:
        copy.wait()


def ask_kernel(*refs):
    out_ref, owner_ref, cell_ref, polar_ref, azimuth_ref, distance_ref, sem = refs[5:]
    fetch(refs[:5], refs[6:11], sem)
    member = owner_mask(owner_ref[...])
    rank = rank_of(member)
    cell = cell_ref[...]
    low = (cell & 31).astype(F32)
    high = (cell >> 5).astype(F32)
    slot = lax.broadcasted_iota(jnp.int32, (LANES, cell.shape[1]), 0)
    here = jnp.where((slot & 7).astype(F32) == rank, 1.0, 0.0)
    table = here * jnp.where(slot < 8, low, jnp.where(slot < 16, high, 0.0))
    asked = lax.dot_general(
        member.astype(BF16),
        table.astype(BF16),
        (((1,), (1,)), ((), ())),
        preferred_element_type=F32,
    )
    asked = asked + 32.0 * pltpu.roll(asked, LANES - 8, 1)
    lane = lax.broadcasted_iota(jnp.int32, (LANES, LANES), 1)
    polar = polar_ref[...]
    azimuth = azimuth_ref[...]
    distance = distance_ref[...]
    cycle = jnp.sin(polar) * distance
    place = jnp.concatenate(
        [
            jnp.zeros_like(polar),
            cycle * jnp.cos(azimuth),
            cycle * jnp.sin(azimuth),
            distance * jnp.cos(polar),
        ],
        axis=1,
    )
    out_ref[...] = jnp.where(lane < 8, asked, jnp.broadcast_to(place, (LANES, LANES)))


def pick_kernel(ask_ref, values_ref, out_ref, rows_ref):
    wanted = jnp.transpose(ask_ref[...])[0:SLOTS].astype(jnp.int32)
    block = wanted >> 7
    within = wanted & 127
    values = values_ref[...]
    chunks = values.shape[1] // LANES
    for slot in range(SLOTS):
        index = jnp.broadcast_to(within[slot : slot + 1], (16, LANES))
        where = jnp.broadcast_to(block[slot : slot + 1], (16, LANES))
        found = jnp.zeros((16, LANES), F32)
        for chunk in range(chunks):
            part = values[:, chunk * LANES : (chunk + 1) * LANES]
            taken = jnp.take_along_axis(part, index, axis=1)
            found = jnp.where(where == chunk, taken, found)
        rows_ref[slot * 16 : slot * 16 + 16, :] = found
    out_ref[...] = jnp.transpose(rows_ref[...])


def prepare_kernel(harmonic_ref, after_ref, surface_ref, *refs, panel_total):
    values_ref, member_ref, info_ref, panel_ref = refs[5:9]
    rows_ref, owner_ref, polar_ref, azimuth_ref, radius_ref, area_ref, sem = refs[9:]
    sources = list(refs[:5])
    targets = [owner_ref, polar_ref, azimuth_ref, radius_ref, area_ref]
    for var in range(4):
        for which in range(2):
            sources.append(surface_ref.at[var, harmonic_ref[which] - 1])
            targets.append(rows_ref.at[2 * var + which])
    fetch(sources, targets, sem)
    for at in range(8):
        values_ref[2 * at : 2 * at + 2] = rows_ref[at]
    member = owner_mask(owner_ref[...])
    count = member.shape[1]
    member_ref[...] = member.astype(BF16)
    polar = polar_ref[...]
    azimuth = azimuth_ref[...]
    radius = radius_ref[...]
    cycle = jnp.sin(polar)
    normal = (cycle * jnp.cos(azimuth), cycle * jnp.sin(azimuth), jnp.cos(polar))
    line = lax.broadcasted_iota(jnp.int32, (8, count), 0)

    def stack(*rows):
        total = jnp.zeros((8, count), F32)
        for at, value in enumerate(rows):
            total = jnp.where(line == at, value, total)
        return total

    square = stack(
        jnp.ones_like(radius),
        radius * radius,
        *[-2.0 * radius * axis for axis in normal],
    )
    info_ref[0:8] = square
    info_ref[8:16] = stack(jnp.zeros_like(radius), -radius, *normal)
    weight = area_ref[...] * (0.25 / (math.pi * math.sqrt(panel_total)))
    waves = [BASE_WAVE * harmonic_ref[which].astype(F32) for which in range(2)]
    turns = [wave * (1.0 / (2.0 * math.pi)) for wave in waves]
    info_ref[16:24] = stack(rank_of(member), weight, *waves, *turns)

    zero = jnp.zeros((80, count), F32)
    for at, quantity in enumerate((square, info_ref[8:16])):
        high, mid, low = split3(quantity)
        tall = jnp.concatenate([high, mid, high, low, mid, high, zero], axis=0)
        for half in range(count // LANES):
            panel_ref[at, half * LANES : (half + 1) * LANES, :] = jnp.transpose(
                tall[:, half * LANES : (half + 1) * LANES]
            ).astype(BF16)


def observers_kernel(after_ref, ask_ref, observer_ref):
    place = jnp.transpose(ask_ref[...])
    few = lax.broadcasted_iota(jnp.int32, (8, LANES), 0)
    for number in range(32):
        axes = [place[32 * axis + number : 32 * axis + number + 1] for axis in (1, 2, 3)]
        dist = axes[0] * axes[0] + axes[1] * axes[1] + axes[2] * axes[2]
        total = jnp.where(few == 0, dist, jnp.where(few == 1, 1.0, 0.0))
        for at, value in enumerate(axes):
            total = jnp.where(few == at + 2, value, total)
        high, mid, low = split3(total)
        zero = jnp.zeros((80, LANES), F32)
        tall = jnp.concatenate([high, high, mid, high, mid, low, zero], axis=0)
        observer_ref[number // 2, :, (number % 2) * LANES : (number % 2 + 1) * LANES] = tall.astype(BF16)


def radiate_kernel(answer_ref, observer_ref, member_ref, info_ref, *refs):
    square_ref, out_ref, panel_ref, push_ref, even_ref, odd_ref, sums_ref = refs
    count = member_ref.shape[1]
    member = member_ref[...]
    spread = jnp.zeros((LANES, count), F32)
    for part in split3(answer_ref[...]):
        spread = spread + lax.dot_general(
            part.astype(BF16), member, (((0,), (0,)), ((), ())), preferred_element_type=F32
        )
    rank = info_ref[16:17]
    weight = info_ref[17:18]
    picked = jnp.zeros((16, count), F32)
    for slot in range(SLOTS):
        picked = picked + jnp.where(rank == slot, spread[slot * 16 : slot * 16 + 16], 0.0)
    picked = picked * weight
    square = info_ref[0:8]
    offset = info_ref[8:16]
    tall, push = [], []

    def place(number, start, lines):
        at = number * count + start
        panel_ref[at : at + lines.shape[0], :] = lines

    def row(var, which, part):
        at = var * 4 + which * 2 + part
        return picked[at : at + 1]

    for which in range(2):
        wave = info_ref[18 + which : 19 + which]
        flux = [
            wave
            * (
                row(1, which, part) * offset[2:3]
                + row(2, which, part) * offset[3:4]
                + row(3, which, part) * offset[4:5]
            )
            for part in range(2)
        ]
        press = [row(0, which, part) for part in range(2)]
        quantities = [offset * press[0] - square * flux[1], square * flux[0] + offset * press[1]]
        for quantity in quantities:
            high, mid, low = split3(quantity)
            tall += [high, mid, high, low]
        push += [wave * press[0], wave * press[1]]
    tall = jnp.concatenate(tall, axis=0)
    low_lanes = lax.broadcasted_iota(jnp.int32, (LANES, LANES), 1) < 32
    push = jnp.concatenate(push + [jnp.zeros((LANES - 4, count), F32)], axis=0)
    for half in range(count // LANES):
        here = slice(half * LANES, (half + 1) * LANES)
        turned = jnp.transpose(tall[:, here])
        for number in range(4):
            shifted = turned if number == 0 else pltpu.roll(turned, LANES - 32 * number, 1)
            place(number, half * LANES, jnp.where(low_lanes, shifted, 0.0).astype(BF16))
        turned = jnp.transpose(push[:, here])
        for number in range(4):
            push_ref[number, here, :] = jnp.broadcast_to(turned[:, number : number + 1], (LANES, LANES))
    for number in range(2):
        place(4 + number, 0, square_ref[number])

    turns = [jnp.broadcast_to(info_ref[20 + which : 21 + which, 0:LANES], (8, LANES)) for which in range(2)]

    def project(tile, linear_ref):
        linear_ref[...] = jnp.dot(panel_ref[...], observer_ref[tile], preferred_element_type=F32)

    def step(tile, now_ref, later_ref):
        project(jnp.minimum(tile + 1, TILES - 1), later_ref)
        sums = [jnp.zeros((8, LANES), F32)] * 8
        for first in range(0, count, 8):
            rows = slice(first, first + 8)
            push = [push_ref[number, rows, :] for number in range(4)]
            for side in range(2):
                lanes = slice(side * LANES, (side + 1) * LANES)

                def get(number):
                    return now_ref[number * count + first : number * count + first + 8, lanes]

                far = get(4)
                inverse = lax.rsqrt(far)
                distance = far * inverse
                shift = distance * get(5)
                cube = inverse * inverse * inverse
                twice = cube + cube
                for which in range(2):
                    phase = distance * turns[which]
                    phase = phase - ((phase + MAGIC) - MAGIC)
                    z = phase * phase
                    sine = phase * (TAN_TOP[0] + z * TAN_TOP[1])
                    cosine = (z + TAN_LOW[1]) * z + TAN_LOW[0]
                    scale = pl.reciprocal(sine * sine + cosine * cosine, approx=True)
                    part = sine * (scale * twice)
                    sine, cosine = cosine * part, cube - sine * part
                    real = get(2 * which) - shift * push[2 * which + 1]
                    imag = get(2 * which + 1) + shift * push[2 * which]
                    at = 2 * side + 4 * which
                    sums[at] = sums[at] + (cosine * real + sine * imag)
                    sums[at + 1] = sums[at + 1] + (cosine * imag - sine * real)
        for side in range(2):
            for at in range(4):
                line = at * 32 + tile * 2 + side
                value = sums[2 * side + 4 * (at // 2) + at % 2]
                sums_ref[pl.ds(pl.multiple_of(line * 8, 8), 8), :] = value

    project(0, even_ref)

    def one_tile(tile, carry):
        pl.when(tile % 2 == 0)(lambda: step(tile, even_ref, odd_ref))
        pl.when(tile % 2 == 1)(lambda: step(tile, odd_ref, even_ref))
        return carry

    lax.fori_loop(0, TILES, one_tile, 0)
    total = sums_ref[pl.ds(0, LANES, stride=8), :]
    for at in range(1, 8):
        total = total + sums_ref[pl.ds(at, LANES, stride=8), :]
    out_ref[...] = jnp.transpose(total)


def vmem():
    return pl.BlockSpec(memory_space=pltpu.VMEM)


def anywhere():
    return pl.BlockSpec(memory_space=pl.ANY)


def hbm():
    return pl.BlockSpec(memory_space=pltpu.HBM)


def smem():
    return pl.BlockSpec(memory_space=pltpu.SMEM)


def exchange(value):
    return lax.all_to_all(value, "panel", split_axis=0, concat_axis=0, tiled=True)


def local(
    surface,
    fluid_owner,
    cell_row,
    pan_polar,
    pan_azimuth,
    pan_radius,
    pan_area,
    obs_polar,
    obs_azimuth,
    obs_distance,
    harmonic,
):
    per_device = cell_row.shape[0]
    panel_total = per_device * lax.axis_size("panel")
    owner = fluid_owner.reshape(1, per_device)
    table = jax.ShapeDtypeStruct((LANES, LANES), F32)
    params = pltpu.CompilerParams(vmem_limit_bytes=VMEM_LIMIT)
    whole = pltpu.CompilerParams(vmem_limit_bytes=63 * 1024 * 1024)
    line = pltpu.VMEM((1, per_device), F32)
    few = pltpu.VMEM((1, obs_distance.shape[0]), F32)
    names = pltpu.VMEM((1, per_device), jnp.int32)
    ask = pl.pallas_call(
        ask_kernel,
        out_shape=table,
        in_specs=[hbm()] * 5,
        out_specs=vmem(),
        scratch_shapes=[names, names, few, few, few, pltpu.SemaphoreType.DMA((5,))],
        compiler_params=whole,
        name="ask",
    )(
        owner,
        cell_row.reshape(1, per_device),
        obs_polar.reshape(1, -1),
        obs_azimuth.reshape(1, -1),
        obs_distance.reshape(1, -1),
    )
    cells = surface.shape[3]
    values, member, info, square = pl.pallas_call(
        functools.partial(prepare_kernel, panel_total=panel_total),
        out_shape=(
            jax.ShapeDtypeStruct((16, cells), F32),
            jax.ShapeDtypeStruct((LANES, per_device), BF16),
            jax.ShapeDtypeStruct((24, per_device), F32),
            jax.ShapeDtypeStruct((2, per_device, LANES), BF16),
        ),
        in_specs=[smem(), anywhere()] + [hbm()] * 6,
        out_specs=(vmem(),) * 4,
        scratch_shapes=[
            pltpu.VMEM((8, 2, cells), F32),
            names,
            line,
            line,
            line,
            line,
            pltpu.SemaphoreType.DMA((13,)),
        ],
        compiler_params=params,
        cost_estimate=pl.CostEstimate(flops=10**7, bytes_accessed=10**7, transcendentals=0),
        name="prepare",
    )(
        harmonic,
        ask,
        surface,
        owner,
        pan_polar.reshape(1, -1),
        pan_azimuth.reshape(1, -1),
        pan_radius.reshape(1, -1),
        pan_area.reshape(1, -1),
    )
    asked = exchange(ask)
    found = pl.pallas_call(
        pick_kernel,
        out_shape=table,
        in_specs=[vmem()] * 2,
        out_specs=vmem(),
        scratch_shapes=[pltpu.VMEM((LANES, LANES), F32)],
        compiler_params=params,
        name="pick",
    )(asked, values)
    answer = exchange(found)
    pairs = per_device * 32 * LANES
    observer = pl.pallas_call(
        observers_kernel,
        out_shape=jax.ShapeDtypeStruct((TILES, LANES, 2 * LANES), BF16),
        in_specs=[anywhere(), vmem()],
        out_specs=vmem(),
        compiler_params=params,
        cost_estimate=pl.CostEstimate(flops=10**7, bytes_accessed=10**7, transcendentals=0),
        name="observers",
    )(found, asked)
    partial = pl.pallas_call(
        radiate_kernel,
        out_shape=table,
        in_specs=[vmem()] * 5,
        out_specs=vmem(),
        scratch_shapes=[
            pltpu.VMEM((6 * per_device, LANES), BF16),
            pltpu.VMEM((4, per_device, LANES), F32),
            pltpu.VMEM((6 * per_device, 2 * LANES), F32),
            pltpu.VMEM((6 * per_device, 2 * LANES), F32),
            pltpu.VMEM((8 * LANES, LANES), F32),
        ],
        compiler_params=params,
        cost_estimate=pl.CostEstimate(flops=90 * pairs, bytes_accessed=10**6, transcendentals=3 * pairs),
        name="radiate",
    )(answer, observer, member, info, square)
    partial = exchange(partial)
    summed = jnp.sum(partial, axis=0).reshape(2, 2, obs_distance.shape[0])
    return summed * obs_distance[None, None, :]


def solution(mesh):
    in_specs = (
        P(None, None, None, "panel"),
        P("panel", None),
        P("panel"),
        P("panel"),
        P("panel"),
        P("panel"),
        P("panel"),
        P(("panel", "obs")),
        P(("panel", "obs")),
        P(("panel", "obs")),
        P(),
    )
    out_specs = P(None, None, ("panel", "obs"))
    return jax.shard_map(local, mesh=mesh, in_specs=in_specs, out_specs=out_specs, check_vma=False)
```

```python
import functools
import math

import jax
import jax.numpy as jnp
from jax import lax
from jax.experimental import pallas as pl
from jax.experimental.pallas import tpu as pltpu
from jax.sharding import PartitionSpec as P

BASE_WAVE = 2.0
LANES = 128
CHIPS = 64
SLOTS = 16
MAGIC = 12582912.0
F32 = jnp.float32
BF16 = jnp.bfloat16
VMEM_LIMIT = 48 * 1024 * 1024
TILES = 16
JOIN = 1

TAN_TOP = (3.1051745414733887, -2.988323211669922)
TAN_LOW = (0.9884211421012878, -4.203673839569092)


def split3(value):
    high = value.astype(BF16).astype(F32)
    rest = value - high
    mid = rest.astype(BF16).astype(F32)
    return high, mid, rest - mid


def owner_mask(owner):
    rows = lax.broadcasted_iota(jnp.int32, (LANES, owner.shape[1]), 0)
    return jnp.where(rows == owner, 1.0, 0.0).astype(F32)


def rank_of(member):
    count = member.shape[1]
    first = lax.broadcasted_iota(jnp.int32, (count, count), 0)
    second = lax.broadcasted_iota(jnp.int32, (count, count), 1)
    earlier = jnp.where(first < second, 1.0, 0.0).astype(BF16)
    before = jnp.dot(member.astype(BF16), earlier, preferred_element_type=F32)
    return jnp.sum(before * member, axis=0, keepdims=True)


def chip_mask(owner):
    rows = lax.broadcasted_iota(jnp.int32, (CHIPS, owner.shape[1]), 0)
    return jnp.where(rows == (owner >> 1), 1.0, 0.0).astype(F32)


def slot_of(owner):
    return rank_of(owner_mask(owner)) + (8 * (owner & 1)).astype(F32)


def fetch(sources, targets, sem):
    copies = [pltpu.make_async_copy(*pair, sem.at[at]) for at, pair in enumerate(zip(sources, targets))]
    for copy in copies:
        copy.start()
    for copy in copies:
        copy.wait()


def ask_kernel(*refs):
    out_ref, owner_ref, cell_ref, polar_ref, azimuth_ref, distance_ref, sem = refs[5:]
    fetch(refs[:5], refs[6:11], sem)
    owner = owner_ref[...]
    place = slot_of(owner)
    cell = cell_ref[...]
    low = (cell & 31).astype(F32)
    high = (cell >> 5).astype(F32)
    slot = lax.broadcasted_iota(jnp.int32, (LANES, cell.shape[1]), 0)
    here = jnp.where((slot & 15).astype(F32) == place, 1.0, 0.0)
    table = here * jnp.where(slot < 16, low, jnp.where(slot < 32, high, 0.0))
    asked = lax.dot_general(
        chip_mask(owner).astype(BF16),
        table.astype(BF16),
        (((1,), (1,)), ((), ())),
        preferred_element_type=F32,
    )
    asked = asked + 32.0 * pltpu.roll(asked, LANES - 16, 1)
    lane = lax.broadcasted_iota(jnp.int32, (CHIPS, LANES), 1)
    polar = polar_ref[...]
    azimuth = azimuth_ref[...]
    distance = distance_ref[...]
    cycle = jnp.sin(polar) * distance
    place = jnp.concatenate(
        [
            jnp.zeros_like(polar),
            cycle * jnp.cos(azimuth),
            cycle * jnp.sin(azimuth),
            distance * jnp.cos(polar),
        ],
        axis=1,
    )
    out_ref[...] = jnp.where(lane < 16, asked, jnp.broadcast_to(place, (CHIPS, LANES)))


def pick_kernel(ask_ref, own_ref, mate_ref, out_ref, rows_ref):
    square = jnp.concatenate([ask_ref[...], jnp.zeros((LANES - CHIPS, LANES), F32)], axis=0)
    wanted = jnp.transpose(square)[0:SLOTS].astype(jnp.int32)
    block = wanted >> 7
    within = wanted & 127
    first = lax.axis_index("panel") % 2 == 0
    own, mate = own_ref[...], mate_ref[...]
    values = (jnp.where(first, own, mate), jnp.where(first, mate, own))
    chunks = own.shape[1] // LANES
    for slot in range(SLOTS):
        index = jnp.broadcast_to(within[slot : slot + 1], (16, LANES))
        where = jnp.broadcast_to(block[slot : slot + 1], (16, LANES))
        found = jnp.zeros((16, LANES), F32)
        for chunk in range(chunks):
            part = values[slot // 8][:, chunk * LANES : (chunk + 1) * LANES]
            taken = jnp.take_along_axis(part, index, axis=1)
            found = jnp.where(where == chunk, taken, found)
        rows_ref[slot * 16 : slot * 16 + 16, :] = found
    for half in range(2):
        here = slice(half * LANES, (half + 1) * LANES)
        out_ref[pl.ds(half, CHIPS, stride=2), :] = jnp.transpose(rows_ref[here, :])[0:CHIPS]


def prepare_kernel(harmonic_ref, after_ref, surface_ref, *refs, panel_total):
    values_ref, member_ref, info_ref, panel_ref = refs[5:9]
    rows_ref, owner_ref, polar_ref, azimuth_ref, radius_ref, area_ref, sem = refs[9:]
    sources = list(refs[:5])
    targets = [owner_ref, polar_ref, azimuth_ref, radius_ref, area_ref]
    for var in range(4):
        for which in range(2):
            sources.append(surface_ref.at[var, harmonic_ref[which] - 1])
            targets.append(rows_ref.at[2 * var + which])
    fetch(sources, targets, sem)
    for at in range(8):
        values_ref[2 * at : 2 * at + 2] = rows_ref[at]
    owner = owner_ref[...]
    count = owner.shape[1]
    member_ref[...] = chip_mask(owner).astype(BF16)
    polar = polar_ref[...]
    azimuth = azimuth_ref[...]
    radius = radius_ref[...]
    cycle = jnp.sin(polar)
    normal = (cycle * jnp.cos(azimuth), cycle * jnp.sin(azimuth), jnp.cos(polar))
    line = lax.broadcasted_iota(jnp.int32, (8, count), 0)

    def stack(*rows):
        total = jnp.zeros((8, count), F32)
        for at, value in enumerate(rows):
            total = jnp.where(line == at, value, total)
        return total

    square = stack(
        jnp.ones_like(radius),
        radius * radius,
        *[-2.0 * radius * axis for axis in normal],
    )
    info_ref[0:8] = square
    info_ref[8:16] = stack(jnp.zeros_like(radius), -radius, *normal)
    weight = area_ref[...] * (0.25 / (math.pi * math.sqrt(panel_total)))
    waves = [BASE_WAVE * harmonic_ref[which].astype(F32) for which in range(2)]
    turns = [wave * (1.0 / (2.0 * math.pi)) for wave in waves]
    info_ref[16:24] = stack(slot_of(owner), weight, *waves, *turns)

    zero = jnp.zeros((80, count), F32)
    for at, quantity in enumerate((square, info_ref[8:16])):
        high, mid, low = split3(quantity)
        tall = jnp.concatenate([high, mid, high, low, mid, high, zero], axis=0)
        for half in range(count // LANES):
            panel_ref[at, half * LANES : (half + 1) * LANES, :] = jnp.transpose(
                tall[:, half * LANES : (half + 1) * LANES]
            ).astype(BF16)


def observers_kernel(own_ref, mate_ref, observer_ref, distance_ref, rows_ref):
    first = lax.axis_index("panel") % 2 == 0
    own, mate = own_ref[...], mate_ref[...]
    rows_ref[pl.ds(0, CHIPS, stride=2), :] = jnp.where(first, own, mate)
    rows_ref[pl.ds(1, CHIPS, stride=2), :] = jnp.where(first, mate, own)
    place = jnp.transpose(rows_ref[...])
    far = place[32:64] * place[32:64] + place[64:96] * place[64:96] + place[96:128] * place[96:128]
    distance_ref[...] = jnp.sqrt(far)
    few = lax.broadcasted_iota(jnp.int32, (8, LANES), 0)
    for number in range(32):
        axes = [place[32 * axis + number : 32 * axis + number + 1] for axis in (1, 2, 3)]
        total = jnp.where(few == 0, far[number : number + 1], jnp.where(few == 1, 1.0, 0.0))
        for at, value in enumerate(axes):
            total = jnp.where(few == at + 2, value, total)
        high, mid, low = split3(total)
        zero = jnp.zeros((80, LANES), F32)
        tall = jnp.concatenate([high, high, mid, high, mid, low, zero], axis=0)
        observer_ref[number // 2, :, (number % 2) * LANES : (number % 2 + 1) * LANES] = tall.astype(BF16)


def radiate_kernel(answer_ref, observer_ref, distance_ref, member_ref, info_ref, *refs):
    square_ref, out_ref, panel_ref, push_ref, even_ref, odd_ref, sums_ref = refs
    count = member_ref.shape[1]
    member = member_ref[...]
    spread = [jnp.zeros((LANES, count), F32)] * 2
    for half in range(2):
        for part in split3(answer_ref[pl.ds(half, CHIPS, stride=2), :]):
            spread[half] = spread[half] + lax.dot_general(
                part.astype(BF16), member, (((0,), (0,)), ((), ())), preferred_element_type=F32
            )
    rank = info_ref[16:17]
    weight = info_ref[17:18]
    picked = jnp.zeros((16, count), F32)
    for slot in range(SLOTS):
        lines = spread[slot // 8][slot % 8 * 16 : slot % 8 * 16 + 16]
        picked = picked + jnp.where(rank == slot, lines, 0.0)
    picked = picked * weight
    square = info_ref[0:8]
    offset = info_ref[8:16]
    tall, push = [], []

    def place(number, start, lines):
        at = number * count + start
        panel_ref[at : at + lines.shape[0], :] = lines

    def row(var, which, part):
        at = var * 4 + which * 2 + part
        return picked[at : at + 1]

    for which in range(2):
        wave = info_ref[18 + which : 19 + which]
        flux = [
            wave
            * (
                row(1, which, part) * offset[2:3]
                + row(2, which, part) * offset[3:4]
                + row(3, which, part) * offset[4:5]
            )
            for part in range(2)
        ]
        press = [row(0, which, part) for part in range(2)]
        quantities = [offset * press[0] - square * flux[1], square * flux[0] + offset * press[1]]
        for quantity in quantities:
            high, mid, low = split3(quantity)
            tall += [high, mid, high, low]
        push += [wave * press[0], wave * press[1]]
    tall = jnp.concatenate(tall, axis=0)
    low_lanes = lax.broadcasted_iota(jnp.int32, (LANES, LANES), 1) < 32
    push = jnp.concatenate(push + [jnp.zeros((LANES - 4, count), F32)], axis=0)
    for half in range(count // LANES):
        here = slice(half * LANES, (half + 1) * LANES)
        turned = jnp.transpose(tall[:, here])
        for number in range(4):
            shifted = turned if number == 0 else pltpu.roll(turned, LANES - 32 * number, 1)
            place(number, half * LANES, jnp.where(low_lanes, shifted, 0.0).astype(BF16))
        turned = jnp.transpose(push[:, here])
        for number in range(4):
            push_ref[number, here, :] = jnp.broadcast_to(turned[:, number : number + 1], (LANES, LANES))
    for number in range(2):
        place(4 + number, 0, square_ref[number])

    turns = [jnp.broadcast_to(info_ref[20 + which : 21 + which, 0:LANES], (8, LANES)) for which in range(2)]

    def project(step, linear_ref):
        views = jnp.concatenate([observer_ref[step * JOIN + at] for at in range(JOIN)], axis=1)
        linear_ref[...] = jnp.dot(panel_ref[...], views, preferred_element_type=F32)

    def tiles(step, now_ref, later_ref):
        for side in range(2 * JOIN):
            lanes = slice(side * LANES, (side + 1) * LANES)
            sums = [jnp.zeros((8, LANES), F32)] * 4
            for first in range(0, count, 8):
                if first % 64 == 0 and side * 4 + first // 64 < 6:
                    number = side * 4 + first // 64
                    lines = pl.ds(number * count, count)
                    following = observer_ref[jnp.minimum(step + 1, TILES // JOIN - 1)]
                    later_ref[lines, :] = jnp.dot(panel_ref[lines, :], following, preferred_element_type=F32)
                rows = slice(first, first + 8)

                def get(number):
                    return now_ref[number * count + first : number * count + first + 8, lanes]

                far = get(4)
                inverse = lax.rsqrt(far)
                distance = far * inverse
                shift = distance * get(5)
                cube = inverse * inverse * inverse
                twice = cube + cube
                for which in range(2):
                    phase = distance * turns[which]
                    phase = phase - jnp.round(phase)
                    z = phase * phase
                    sine = phase * (TAN_TOP[0] + z * TAN_TOP[1])
                    cosine = (z + TAN_LOW[1]) * z + TAN_LOW[0]
                    scale = pl.reciprocal(sine * sine + cosine * cosine, approx=True)
                    part = sine * (scale * twice)
                    sine, cosine = cosine * part, cube - sine * part
                    real = get(2 * which) - shift * push_ref[2 * which + 1, rows, :]
                    imag = get(2 * which + 1) + shift * push_ref[2 * which, rows, :]
                    sums[2 * which] = sums[2 * which] + (cosine * real + sine * imag)
                    sums[2 * which + 1] = sums[2 * which + 1] + (cosine * imag - sine * real)
            for at in range(4):
                line = at * 32 + step * 2 * JOIN + side
                sums_ref[pl.ds(pl.multiple_of(line * 8, 8), 8), :] = sums[at]

    project(0, even_ref)

    def one_step(step, carry):
        pl.when(step % 2 == 0)(lambda: tiles(step, even_ref, odd_ref))
        pl.when(step % 2 == 1)(lambda: tiles(step, odd_ref, even_ref))
        return carry

    lax.fori_loop(0, TILES // JOIN, one_step, 0)
    total = sums_ref[pl.ds(0, LANES, stride=8), :]
    for at in range(1, 8):
        total = total + sums_ref[pl.ds(at, LANES, stride=8), :]
    total = total * jnp.concatenate([distance_ref[...]] * 4, axis=0)
    out_ref[...] = jnp.transpose(total)


def vmem():
    return pl.BlockSpec(memory_space=pltpu.VMEM)


def anywhere():
    return pl.BlockSpec(memory_space=pl.ANY)


def hbm():
    return pl.BlockSpec(memory_space=pltpu.HBM)


def smem():
    return pl.BlockSpec(memory_space=pltpu.SMEM)


SAME_CORE = [[2 * chip + core for chip in range(CHIPS)] for core in range(2)]


def exchange(value, groups=None):
    return lax.all_to_all(
        value, "panel", split_axis=0, concat_axis=0, axis_index_groups=groups, tiled=True
    )


def swap(value):
    return lax.ppermute(value, "panel", [(at, at ^ 1) for at in range(2 * CHIPS)])


def local(
    surface,
    fluid_owner,
    cell_row,
    pan_polar,
    pan_azimuth,
    pan_radius,
    pan_area,
    obs_polar,
    obs_azimuth,
    obs_distance,
    harmonic,
):
    per_device = cell_row.shape[0]
    panel_total = per_device * lax.axis_size("panel")
    owner = fluid_owner.reshape(1, per_device)
    table = jax.ShapeDtypeStruct((LANES, LANES), F32)
    params = pltpu.CompilerParams(vmem_limit_bytes=VMEM_LIMIT)
    whole = pltpu.CompilerParams(vmem_limit_bytes=63 * 1024 * 1024)
    line = pltpu.VMEM((1, per_device), F32)
    few = pltpu.VMEM((1, obs_distance.shape[0]), F32)
    names = pltpu.VMEM((1, per_device), jnp.int32)
    ask = pl.pallas_call(
        ask_kernel,
        out_shape=jax.ShapeDtypeStruct((CHIPS, LANES), F32),
        in_specs=[hbm()] * 5,
        out_specs=vmem(),
        scratch_shapes=[names, names, few, few, few, pltpu.SemaphoreType.DMA((5,))],
        compiler_params=whole,
        name="ask",
    )(
        owner,
        cell_row.reshape(1, per_device),
        obs_polar.reshape(1, -1),
        obs_azimuth.reshape(1, -1),
        obs_distance.reshape(1, -1),
    )
    cells = surface.shape[3]
    values, member, info, square = pl.pallas_call(
        functools.partial(prepare_kernel, panel_total=panel_total),
        out_shape=(
            jax.ShapeDtypeStruct((16, cells), F32),
            jax.ShapeDtypeStruct((CHIPS, per_device), BF16),
            jax.ShapeDtypeStruct((24, per_device), F32),
            jax.ShapeDtypeStruct((2, per_device, LANES), BF16),
        ),
        in_specs=[smem(), anywhere()] + [hbm()] * 6,
        out_specs=(vmem(),) * 4,
        scratch_shapes=[
            pltpu.VMEM((8, 2, cells), F32),
            names,
            line,
            line,
            line,
            line,
            pltpu.SemaphoreType.DMA((13,)),
        ],
        compiler_params=params,
        cost_estimate=pl.CostEstimate(flops=10**7, bytes_accessed=10**7, transcendentals=0),
        name="prepare",
    )(
        harmonic,
        ask,
        surface,
        owner,
        pan_polar.reshape(1, -1),
        pan_azimuth.reshape(1, -1),
        pan_radius.reshape(1, -1),
        pan_area.reshape(1, -1),
    )
    mate_values = swap(values)
    asked = exchange(ask, SAME_CORE)
    found = pl.pallas_call(
        pick_kernel,
        out_shape=table,
        in_specs=[vmem()] * 3,
        out_specs=vmem(),
        scratch_shapes=[pltpu.VMEM((SLOTS * 16, LANES), F32)],
        compiler_params=params,
        name="pick",
    )(asked, values, mate_values)
    answer = exchange(found, SAME_CORE)
    asked, _ = lax.optimization_barrier((asked, found))
    mate_asked = swap(asked)
    pairs = per_device * 32 * LANES
    observer, distance = pl.pallas_call(
        observers_kernel,
        out_shape=(
            jax.ShapeDtypeStruct((TILES, LANES, 2 * LANES), BF16),
            jax.ShapeDtypeStruct((32, LANES), F32),
        ),
        in_specs=[vmem()] * 2,
        out_specs=(vmem(),) * 2,
        scratch_shapes=[pltpu.VMEM((LANES, LANES), F32)],
        compiler_params=params,
        cost_estimate=pl.CostEstimate(flops=10**7, bytes_accessed=10**7, transcendentals=0),
        name="observers",
    )(asked, mate_asked)
    partial = pl.pallas_call(
        radiate_kernel,
        out_shape=table,
        in_specs=[vmem()] * 6,
        out_specs=vmem(),
        scratch_shapes=[
            pltpu.VMEM((6 * per_device, LANES), BF16),
            pltpu.VMEM((4, per_device, LANES), F32),
            pltpu.VMEM((6 * per_device, 2 * JOIN * LANES), F32),
            pltpu.VMEM((6 * per_device, 2 * JOIN * LANES), F32),
            pltpu.VMEM((8 * LANES, LANES), F32),
        ],
        compiler_params=params,
        cost_estimate=pl.CostEstimate(flops=90 * pairs, bytes_accessed=10**6, transcendentals=3 * pairs),
        name="radiate",
    )(answer, observer, distance, member, info, square)
    partial = exchange(partial)
    return jnp.sum(partial, axis=0).reshape(2, 2, obs_distance.shape[0])


def solution(mesh):
    in_specs = (
        P(None, None, None, "panel"),
        P("panel", None),
        P("panel"),
        P("panel"),
        P("panel"),
        P("panel"),
        P("panel"),
        P(("panel", "obs")),
        P(("panel", "obs")),
        P(("panel", "obs")),
        P(),
    )
    out_specs = P(None, None, ("panel", "obs"))
    return jax.shard_map(local, mesh=mesh, in_specs=in_specs, out_specs=out_specs, check_vma=False)
```

```python
import functools
import math

import jax
import jax.numpy as jnp
from jax import lax
from jax.experimental import pallas as pl
from jax.experimental.pallas import tpu as pltpu
from jax.sharding import PartitionSpec as P

BASE_WAVE = 2.0
LANES = 128
CHIPS = 64
FIRST = 40
SLOTS = 16
MAGIC = 12582912.0
F32 = jnp.float32
BF16 = jnp.bfloat16
VMEM_LIMIT = 48 * 1024 * 1024
TILES = 16
JOIN = 1

TAN_TOP = (3.1051745414733887, -2.988323211669922)
TAN_LOW = (0.9884211421012878, -4.203673839569092)


def split3(value):
    high = value.astype(BF16).astype(F32)
    rest = value - high
    mid = rest.astype(BF16).astype(F32)
    return high, mid, rest - mid


def owner_mask(owner):
    rows = lax.broadcasted_iota(jnp.int32, (LANES, owner.shape[1]), 0)
    return jnp.where(rows == owner, 1.0, 0.0).astype(F32)


def rank_of(member):
    count = member.shape[1]
    first = lax.broadcasted_iota(jnp.int32, (count, count), 0)
    second = lax.broadcasted_iota(jnp.int32, (count, count), 1)
    earlier = jnp.where(first < second, 1.0, 0.0).astype(BF16)
    before = jnp.dot(member.astype(BF16), earlier, preferred_element_type=F32)
    return jnp.sum(before * member, axis=0, keepdims=True)


def chip_mask(owner):
    rows = lax.broadcasted_iota(jnp.int32, (CHIPS, owner.shape[1]), 0)
    return jnp.where(rows == ((owner >> 1) + CHIPS - FIRST) % CHIPS, 1.0, 0.0).astype(F32)


def slot_of(owner):
    return rank_of(owner_mask(owner)) + (8 * (owner & 1)).astype(F32)


def fetch(sources, targets, sem):
    copies = [pltpu.make_async_copy(*pair, sem.at[at]) for at, pair in enumerate(zip(sources, targets))]
    for copy in copies:
        copy.start()
    for copy in copies:
        copy.wait()


def ask_kernel(*refs):
    out_ref, owner_ref, cell_ref, polar_ref, azimuth_ref, distance_ref, sem = refs[5:]
    fetch(refs[:5], refs[6:11], sem)
    owner = owner_ref[...]
    place = slot_of(owner)
    cell = cell_ref[...]
    low = (cell & 31).astype(F32)
    high = (cell >> 5).astype(F32)
    slot = lax.broadcasted_iota(jnp.int32, (LANES, cell.shape[1]), 0)
    here = jnp.where((slot & 15).astype(F32) == place, 1.0, 0.0)
    table = here * jnp.where(slot < 16, low, jnp.where(slot < 32, high, 0.0))
    asked = lax.dot_general(
        chip_mask(owner).astype(BF16),
        table.astype(BF16),
        (((1,), (1,)), ((), ())),
        preferred_element_type=F32,
    )
    asked = asked + 32.0 * pltpu.roll(asked, LANES - 16, 1)
    lane = lax.broadcasted_iota(jnp.int32, (CHIPS, LANES), 1)
    polar = polar_ref[...]
    azimuth = azimuth_ref[...]
    distance = distance_ref[...]
    cycle = jnp.sin(polar) * distance
    place = jnp.concatenate(
        [
            jnp.zeros_like(polar),
            cycle * jnp.cos(azimuth),
            cycle * jnp.sin(azimuth),
            distance * jnp.cos(polar),
        ],
        axis=1,
    )
    out_ref[...] = jnp.where(lane < 16, asked, jnp.broadcast_to(place, (CHIPS, LANES)))


def pick_kernel(ask_ref, own_ref, mate_ref, out_ref, rows_ref):
    square = jnp.concatenate([ask_ref[...], jnp.zeros((LANES - CHIPS, LANES), F32)], axis=0)
    wanted = jnp.transpose(square)[0:SLOTS].astype(jnp.int32)
    block = wanted >> 7
    within = wanted & 127
    first = lax.axis_index("panel") % 2 == 0
    own, mate = [
        jnp.concatenate([ref[at] for at in range(8)], axis=0) for ref in (own_ref, mate_ref)
    ]
    values = (jnp.where(first, own, mate), jnp.where(first, mate, own))
    chunks = own.shape[1] // LANES
    for slot in range(SLOTS):
        index = jnp.broadcast_to(within[slot : slot + 1], (16, LANES))
        where = jnp.broadcast_to(block[slot : slot + 1], (16, LANES))
        found = jnp.zeros((16, LANES), F32)
        for chunk in range(chunks):
            part = values[slot // 8][:, chunk * LANES : (chunk + 1) * LANES]
            taken = jnp.take_along_axis(part, index, axis=1)
            found = jnp.where(where == chunk, taken, found)
        rows_ref[slot * 16 : slot * 16 + 16, :] = found
    for half in range(2):
        here = slice(half * LANES, (half + 1) * LANES)
        out_ref[pl.ds(half, CHIPS, stride=2), :] = jnp.transpose(rows_ref[here, :])[0:CHIPS]


def select_kernel(harmonic_ref, after_ref, surface_ref, out_ref, sem):
    sources, targets = [], []
    for var in range(4):
        for which in range(2):
            sources.append(surface_ref.at[var, harmonic_ref[which] - 1])
            targets.append(out_ref.at[2 * var + which])
    fetch(sources, targets, sem)


def prepare_kernel(harmonic_ref, after_ref, *refs, panel_total):
    owner_ref, polar_ref, azimuth_ref, radius_ref, area_ref, member_ref, info_ref, panel_ref = refs
    owner = owner_ref[...]
    count = owner.shape[1]
    member_ref[...] = chip_mask(owner).astype(BF16)
    polar = polar_ref[...]
    azimuth = azimuth_ref[...]
    radius = radius_ref[...]
    cycle = jnp.sin(polar)
    normal = (cycle * jnp.cos(azimuth), cycle * jnp.sin(azimuth), jnp.cos(polar))
    line = lax.broadcasted_iota(jnp.int32, (8, count), 0)

    def stack(*rows):
        total = jnp.zeros((8, count), F32)
        for at, value in enumerate(rows):
            total = jnp.where(line == at, value, total)
        return total

    square = stack(
        jnp.ones_like(radius),
        radius * radius,
        *[-2.0 * radius * axis for axis in normal],
    )
    info_ref[0:8] = square
    info_ref[8:16] = stack(jnp.zeros_like(radius), -radius, *normal)
    weight = area_ref[...] * (0.25 / (math.pi * math.sqrt(panel_total)))
    waves = [BASE_WAVE * harmonic_ref[which].astype(F32) for which in range(2)]
    turns = [wave * (1.0 / (2.0 * math.pi)) for wave in waves]
    info_ref[16:24] = stack(slot_of(owner), weight, *waves, *turns)

    zero = jnp.zeros((80, count), F32)
    for at, quantity in enumerate((square, info_ref[8:16])):
        high, mid, low = split3(quantity)
        tall = jnp.concatenate([high, mid, high, low, mid, high, zero], axis=0)
        for half in range(count // LANES):
            panel_ref[at, half * LANES : (half + 1) * LANES, :] = jnp.transpose(
                tall[:, half * LANES : (half + 1) * LANES]
            ).astype(BF16)


def observers_kernel(own_ref, mate_ref, observer_ref, distance_ref, rows_ref):
    first = lax.axis_index("panel") % 2 == 0
    own, mate = own_ref[...], mate_ref[...]
    rows_ref[pl.ds(0, CHIPS, stride=2), :] = jnp.where(first, own, mate)
    rows_ref[pl.ds(1, CHIPS, stride=2), :] = jnp.where(first, mate, own)
    place = jnp.transpose(rows_ref[...])
    far = place[32:64] * place[32:64] + place[64:96] * place[64:96] + place[96:128] * place[96:128]
    distance_ref[...] = jnp.sqrt(far)
    few = lax.broadcasted_iota(jnp.int32, (8, LANES), 0)
    for number in range(32):
        axes = [place[32 * axis + number : 32 * axis + number + 1] for axis in (1, 2, 3)]
        total = jnp.where(few == 0, far[number : number + 1], jnp.where(few == 1, 1.0, 0.0))
        for at, value in enumerate(axes):
            total = jnp.where(few == at + 2, value, total)
        high, mid, low = split3(total)
        zero = jnp.zeros((80, LANES), F32)
        tall = jnp.concatenate([high, high, mid, high, mid, low, zero], axis=0)
        observer_ref[number // 2, :, (number % 2) * LANES : (number % 2 + 1) * LANES] = tall.astype(BF16)


def radiate_kernel(answer_ref, observer_ref, distance_ref, member_ref, info_ref, *refs):
    square_ref, out_ref, panel_ref, push_ref, even_ref, odd_ref, sums_ref = refs
    count = member_ref.shape[1]
    member = member_ref[...]
    spread = [jnp.zeros((LANES, count), F32)] * 2
    for half in range(2):
        for part in split3(answer_ref[pl.ds(half, CHIPS, stride=2), :]):
            spread[half] = spread[half] + lax.dot_general(
                part.astype(BF16), member, (((0,), (0,)), ((), ())), preferred_element_type=F32
            )
    rank = info_ref[16:17]
    weight = info_ref[17:18]
    picked = jnp.zeros((16, count), F32)
    for slot in range(SLOTS):
        lines = spread[slot // 8][slot % 8 * 16 : slot % 8 * 16 + 16]
        picked = picked + jnp.where(rank == slot, lines, 0.0)
    picked = picked * weight
    square = info_ref[0:8]
    offset = info_ref[8:16]
    tall, push = [], []

    def place(number, start, lines):
        at = number * count + start
        panel_ref[at : at + lines.shape[0], :] = lines

    def row(var, which, part):
        at = var * 4 + which * 2 + part
        return picked[at : at + 1]

    for which in range(2):
        wave = info_ref[18 + which : 19 + which]
        flux = [
            wave
            * (
                row(1, which, part) * offset[2:3]
                + row(2, which, part) * offset[3:4]
                + row(3, which, part) * offset[4:5]
            )
            for part in range(2)
        ]
        press = [row(0, which, part) for part in range(2)]
        quantities = [offset * press[0] - square * flux[1], square * flux[0] + offset * press[1]]
        for quantity in quantities:
            high, mid, low = split3(quantity)
            tall += [high, mid, high, low]
        push += [wave * press[0], wave * press[1]]
    tall = jnp.concatenate(tall, axis=0)
    low_lanes = lax.broadcasted_iota(jnp.int32, (LANES, LANES), 1) < 32
    push = jnp.concatenate(push + [jnp.zeros((LANES - 4, count), F32)], axis=0)
    for half in range(count // LANES):
        here = slice(half * LANES, (half + 1) * LANES)
        turned = jnp.transpose(tall[:, here])
        for number in range(4):
            shifted = turned if number == 0 else pltpu.roll(turned, LANES - 32 * number, 1)
            place(number, half * LANES, jnp.where(low_lanes, shifted, 0.0).astype(BF16))
        turned = jnp.transpose(push[:, here])
        for number in range(4):
            push_ref[number, here, :] = jnp.broadcast_to(turned[:, number : number + 1], (LANES, LANES))
    for number in range(2):
        place(4 + number, 0, square_ref[number])

    turns = [jnp.broadcast_to(info_ref[20 + which : 21 + which, 0:LANES], (8, LANES)) for which in range(2)]

    def project(step, linear_ref):
        views = jnp.concatenate([observer_ref[step * JOIN + at] for at in range(JOIN)], axis=1)
        linear_ref[...] = jnp.dot(panel_ref[...], views, preferred_element_type=F32)

    def tiles(step, now_ref, later_ref):
        for side in range(2 * JOIN):
            lanes = slice(side * LANES, (side + 1) * LANES)
            sums = [jnp.zeros((8, LANES), F32)] * 4
            for first in range(0, count, 8):
                if first % 64 == 0 and side * 4 + first // 64 < 6:
                    number = side * 4 + first // 64
                    lines = pl.ds(number * count, count)
                    following = observer_ref[jnp.minimum(step + 1, TILES // JOIN - 1)]
                    later_ref[lines, :] = jnp.dot(panel_ref[lines, :], following, preferred_element_type=F32)
                rows = slice(first, first + 8)

                def get(number):
                    return now_ref[number * count + first : number * count + first + 8, lanes]

                far = get(4)
                inverse = lax.rsqrt(far)
                distance = far * inverse
                shift = distance * get(5)
                cube = inverse * inverse * inverse
                twice = cube + cube
                for which in range(2):
                    phase = distance * turns[which]
                    phase = phase - jnp.round(phase)
                    z = phase * phase
                    sine = phase * (TAN_TOP[0] + z * TAN_TOP[1])
                    cosine = (z + TAN_LOW[1]) * z + TAN_LOW[0]
                    scale = pl.reciprocal(sine * sine + cosine * cosine, approx=True)
                    part = sine * (scale * twice)
                    sine, cosine = cosine * part, cube - sine * part
                    real = get(2 * which) - shift * push_ref[2 * which + 1, rows, :]
                    imag = get(2 * which + 1) + shift * push_ref[2 * which, rows, :]
                    sums[2 * which] = sums[2 * which] + (cosine * real + sine * imag)
                    sums[2 * which + 1] = sums[2 * which + 1] + (cosine * imag - sine * real)
            for at in range(4):
                line = at * 32 + step * 2 * JOIN + side
                sums_ref[pl.ds(pl.multiple_of(line * 8, 8), 8), :] = sums[at]

    project(0, even_ref)

    def one_step(step, carry):
        pl.when(step % 2 == 0)(lambda: tiles(step, even_ref, odd_ref))
        pl.when(step % 2 == 1)(lambda: tiles(step, odd_ref, even_ref))
        return carry

    lax.fori_loop(0, TILES // JOIN, one_step, 0)
    total = sums_ref[pl.ds(0, LANES, stride=8), :]
    for at in range(1, 8):
        total = total + sums_ref[pl.ds(at, LANES, stride=8), :]
    total = total * jnp.concatenate([distance_ref[...]] * 4, axis=0)
    out_ref[...] = jnp.transpose(total)


def vmem():
    return pl.BlockSpec(memory_space=pltpu.VMEM)


def anywhere():
    return pl.BlockSpec(memory_space=pl.ANY)


def hbm():
    return pl.BlockSpec(memory_space=pltpu.HBM)


def smem():
    return pl.BlockSpec(memory_space=pltpu.SMEM)


ORDER = [(FIRST + at) % CHIPS for at in range(CHIPS)]
SAME_CORE = [[2 * chip + core for chip in ORDER] for core in range(2)]
ALL_CORES = [[2 * chip + core for chip in ORDER for core in range(2)]]


def exchange(value, groups):
    return lax.all_to_all(
        value, "panel", split_axis=0, concat_axis=0, axis_index_groups=groups, tiled=True
    )


def swap(value):
    return lax.ppermute(value, "panel", [(at, at ^ 1) for at in range(2 * CHIPS)])


def local(
    surface,
    fluid_owner,
    cell_row,
    pan_polar,
    pan_azimuth,
    pan_radius,
    pan_area,
    obs_polar,
    obs_azimuth,
    obs_distance,
    harmonic,
):
    per_device = cell_row.shape[0]
    panel_total = per_device * lax.axis_size("panel")
    owner = fluid_owner.reshape(1, per_device)
    table = jax.ShapeDtypeStruct((LANES, LANES), F32)
    params = pltpu.CompilerParams(vmem_limit_bytes=VMEM_LIMIT)
    whole = pltpu.CompilerParams(vmem_limit_bytes=63 * 1024 * 1024)
    line = pltpu.VMEM((1, per_device), F32)
    few = pltpu.VMEM((1, obs_distance.shape[0]), F32)
    names = pltpu.VMEM((1, per_device), jnp.int32)
    ask = pl.pallas_call(
        ask_kernel,
        out_shape=jax.ShapeDtypeStruct((CHIPS, LANES), F32),
        in_specs=[hbm()] * 5,
        out_specs=vmem(),
        scratch_shapes=[names, names, few, few, few, pltpu.SemaphoreType.DMA((5,))],
        compiler_params=whole,
        name="ask",
    )(
        owner,
        cell_row.reshape(1, per_device),
        obs_polar.reshape(1, -1),
        obs_azimuth.reshape(1, -1),
        obs_distance.reshape(1, -1),
    )
    values = pl.pallas_call(
        select_kernel,
        out_shape=jax.ShapeDtypeStruct((8, 2, surface.shape[3]), F32),
        in_specs=[smem(), anywhere(), hbm()],
        out_specs=vmem(),
        scratch_shapes=[pltpu.SemaphoreType.DMA((8,))],
        compiler_params=params,
        cost_estimate=pl.CostEstimate(flops=10**7, bytes_accessed=10**7, transcendentals=0),
        name="select",
    )(harmonic, ask, surface)
    mate_values = swap(values)
    asked = exchange(ask, SAME_CORE)
    found = pl.pallas_call(
        pick_kernel,
        out_shape=table,
        in_specs=[vmem()] * 3,
        out_specs=vmem(),
        scratch_shapes=[pltpu.VMEM((SLOTS * 16, LANES), F32)],
        compiler_params=params,
        name="pick",
    )(asked, values, mate_values)
    answer = exchange(found, SAME_CORE)
    asked, _ = lax.optimization_barrier((asked, found))
    mate_asked = swap(asked)
    member, info, square = pl.pallas_call(
        functools.partial(prepare_kernel, panel_total=panel_total),
        out_shape=(
            jax.ShapeDtypeStruct((CHIPS, per_device), BF16),
            jax.ShapeDtypeStruct((24, per_device), F32),
            jax.ShapeDtypeStruct((2, per_device, LANES), BF16),
        ),
        in_specs=[smem(), anywhere()] + [vmem()] * 5,
        out_specs=(vmem(),) * 3,
        compiler_params=params,
        cost_estimate=pl.CostEstimate(flops=10**7, bytes_accessed=10**7, transcendentals=0),
        name="prepare",
    )(
        harmonic,
        found,
        owner,
        pan_polar.reshape(1, -1),
        pan_azimuth.reshape(1, -1),
        pan_radius.reshape(1, -1),
        pan_area.reshape(1, -1),
    )
    pairs = per_device * 32 * LANES
    observer, distance = pl.pallas_call(
        observers_kernel,
        out_shape=(
            jax.ShapeDtypeStruct((TILES, LANES, 2 * LANES), BF16),
            jax.ShapeDtypeStruct((32, LANES), F32),
        ),
        in_specs=[vmem()] * 2,
        out_specs=(vmem(),) * 2,
        scratch_shapes=[pltpu.VMEM((LANES, LANES), F32)],
        compiler_params=params,
        cost_estimate=pl.CostEstimate(flops=10**7, bytes_accessed=10**7, transcendentals=0),
        name="observers",
    )(asked, mate_asked)
    partial = pl.pallas_call(
        radiate_kernel,
        out_shape=table,
        in_specs=[vmem()] * 6,
        out_specs=vmem(),
        scratch_shapes=[
            pltpu.VMEM((6 * per_device, LANES), BF16),
            pltpu.VMEM((4, per_device, LANES), F32),
            pltpu.VMEM((6 * per_device, 2 * JOIN * LANES), F32),
            pltpu.VMEM((6 * per_device, 2 * JOIN * LANES), F32),
            pltpu.VMEM((8 * LANES, LANES), F32),
        ],
        compiler_params=params,
        cost_estimate=pl.CostEstimate(flops=90 * pairs, bytes_accessed=10**6, transcendentals=3 * pairs),
        name="radiate",
    )(answer, observer, distance, member, info, square)
    partial = exchange(partial, ALL_CORES)
    return jnp.sum(partial, axis=0).reshape(2, 2, obs_distance.shape[0])


def solution(mesh):
    in_specs = (
        P(None, None, None, "panel"),
        P("panel", None),
        P("panel"),
        P("panel"),
        P("panel"),
        P("panel"),
        P("panel"),
        P(("panel", "obs")),
        P(("panel", "obs")),
        P(("panel", "obs")),
        P(),
    )
    out_specs = P(None, None, ("panel", "obs"))
    return jax.shard_map(local, mesh=mesh, in_specs=in_specs, out_specs=out_specs, check_vma=False)
```

```python
import functools
import math

import jax
import jax.numpy as jnp
from jax import lax
from jax.experimental import pallas as pl
from jax.experimental.pallas import tpu as pltpu
from jax.sharding import PartitionSpec as P

BASE_WAVE = 2.0
LANES = 128
CHIPS = 64
FIRST = 40
SLOTS = 16
MAGIC = 12582912.0
F32 = jnp.float32
BF16 = jnp.bfloat16
VMEM_LIMIT = 48 * 1024 * 1024
TILES = 16
JOIN = 1

TAN_TOP = (3.1051745414733887, -2.988323211669922)
TAN_LOW = (0.9884211421012878, -4.203673839569092)


def split3(value):
    high = value.astype(BF16).astype(F32)
    rest = value - high
    mid = rest.astype(BF16).astype(F32)
    return high, mid, rest - mid


def owner_mask(owner):
    rows = lax.broadcasted_iota(jnp.int32, (LANES, owner.shape[1]), 0)
    return jnp.where(rows == owner, 1.0, 0.0).astype(F32)


def rank_of(member):
    count = member.shape[1]
    first = lax.broadcasted_iota(jnp.int32, (count, count), 0)
    second = lax.broadcasted_iota(jnp.int32, (count, count), 1)
    earlier = jnp.where(first < second, 1.0, 0.0).astype(BF16)
    before = jnp.dot(member.astype(BF16), earlier, preferred_element_type=F32)
    return jnp.sum(before * member, axis=0, keepdims=True)


def chip_mask(owner):
    rows = lax.broadcasted_iota(jnp.int32, (CHIPS, owner.shape[1]), 0)
    return jnp.where(rows == ((owner >> 1) + CHIPS - FIRST) % CHIPS, 1.0, 0.0).astype(F32)


def slot_of(owner):
    return rank_of(owner_mask(owner)) + (8 * (owner & 1)).astype(F32)


def fetch(sources, targets, sem):
    copies = [pltpu.make_async_copy(*pair, sem.at[at]) for at, pair in enumerate(zip(sources, targets))]
    for copy in copies:
        copy.start()
    for copy in copies:
        copy.wait()


def ask_kernel(*refs):
    out_ref, owner_ref, cell_ref, polar_ref, azimuth_ref, distance_ref, sem = refs[5:]
    fetch(refs[:5], refs[6:11], sem)
    owner = owner_ref[...]
    place = slot_of(owner)
    cell = cell_ref[...]
    low = (cell & 31).astype(F32)
    high = (cell >> 5).astype(F32)
    slot = lax.broadcasted_iota(jnp.int32, (LANES, cell.shape[1]), 0)
    here = jnp.where((slot & 15).astype(F32) == place, 1.0, 0.0)
    table = here * jnp.where(slot < 16, low, jnp.where(slot < 32, high, 0.0))
    asked = lax.dot_general(
        chip_mask(owner).astype(BF16),
        table.astype(BF16),
        (((1,), (1,)), ((), ())),
        preferred_element_type=F32,
    )
    asked = asked + 32.0 * pltpu.roll(asked, LANES - 16, 1)
    lane = lax.broadcasted_iota(jnp.int32, (CHIPS, LANES), 1)
    polar = polar_ref[...]
    azimuth = azimuth_ref[...]
    distance = distance_ref[...]
    cycle = jnp.sin(polar) * distance
    place = jnp.concatenate(
        [
            jnp.zeros_like(polar),
            cycle * jnp.cos(azimuth),
            cycle * jnp.sin(azimuth),
            distance * jnp.cos(polar),
        ],
        axis=1,
    )
    out_ref[...] = jnp.where(lane < 16, asked, jnp.broadcast_to(place, (CHIPS, LANES)))


def pick_kernel(ask_ref, own_ref, mate_ref, out_ref, rows_ref):
    square = jnp.concatenate([ask_ref[...], jnp.zeros((LANES - CHIPS, LANES), F32)], axis=0)
    wanted = jnp.transpose(square)[0:SLOTS].astype(jnp.int32)
    block = wanted >> 7
    within = wanted & 127
    first = lax.axis_index("panel") % 2 == 0
    own, mate = [
        jnp.concatenate([ref[at] for at in range(8)], axis=0) for ref in (own_ref, mate_ref)
    ]
    values = (jnp.where(first, own, mate), jnp.where(first, mate, own))
    chunks = own.shape[1] // LANES
    for slot in range(SLOTS):
        index = jnp.broadcast_to(within[slot : slot + 1], (16, LANES))
        where = jnp.broadcast_to(block[slot : slot + 1], (16, LANES))
        found = jnp.zeros((16, LANES), F32)
        for chunk in range(chunks):
            part = values[slot // 8][:, chunk * LANES : (chunk + 1) * LANES]
            taken = jnp.take_along_axis(part, index, axis=1)
            found = jnp.where(where == chunk, taken, found)
        rows_ref[slot * 16 : slot * 16 + 16, :] = found
    for half in range(2):
        here = slice(half * LANES, (half + 1) * LANES)
        out_ref[pl.ds(half, CHIPS, stride=2), :] = jnp.transpose(rows_ref[here, :])[0:CHIPS]


def select_kernel(harmonic_ref, after_ref, surface_ref, out_ref, sem):
    sources, targets = [], []
    for var in range(4):
        for which in range(2):
            sources.append(surface_ref.at[var, harmonic_ref[which] - 1])
            targets.append(out_ref.at[2 * var + which])
    fetch(sources, targets, sem)


def prepare_kernel(harmonic_ref, after_ref, *refs, panel_total):
    owner_ref, polar_ref, azimuth_ref, radius_ref, area_ref, member_ref, info_ref, panel_ref = refs
    owner = owner_ref[...]
    count = owner.shape[1]
    member_ref[...] = chip_mask(owner).astype(BF16)
    polar = polar_ref[...]
    azimuth = azimuth_ref[...]
    radius = radius_ref[...]
    cycle = jnp.sin(polar)
    normal = (cycle * jnp.cos(azimuth), cycle * jnp.sin(azimuth), jnp.cos(polar))
    line = lax.broadcasted_iota(jnp.int32, (8, count), 0)

    def stack(*rows):
        total = jnp.zeros((8, count), F32)
        for at, value in enumerate(rows):
            total = jnp.where(line == at, value, total)
        return total

    square = stack(
        jnp.ones_like(radius),
        radius * radius,
        *[-2.0 * radius * axis for axis in normal],
    )
    info_ref[0:8] = square
    info_ref[8:16] = stack(jnp.zeros_like(radius), -radius, *normal)
    weight = area_ref[...] * (0.25 / (math.pi * math.sqrt(panel_total)))
    waves = [BASE_WAVE * harmonic_ref[which].astype(F32) for which in range(2)]
    unit = jnp.full((1, count), waves[0] * (1.0 / (2.0 * math.pi)), F32)
    weight = weight * (unit * unit * unit)
    info_ref[16:24] = stack(slot_of(owner), weight, *waves, 1.0 / unit, waves[1] * ((1.0 / (2.0 * math.pi)) / unit))

    zero = jnp.zeros((80, count), F32)
    for at, quantity in enumerate((square * (unit * unit), info_ref[8:16])):
        high, mid, low = split3(quantity)
        tall = jnp.concatenate([high, mid, high, low, mid, high, zero], axis=0)
        for half in range(count // LANES):
            panel_ref[at, half * LANES : (half + 1) * LANES, :] = jnp.transpose(
                tall[:, half * LANES : (half + 1) * LANES]
            ).astype(BF16)


def observers_kernel(own_ref, mate_ref, observer_ref, distance_ref, rows_ref):
    first = lax.axis_index("panel") % 2 == 0
    own, mate = own_ref[...], mate_ref[...]
    rows_ref[pl.ds(0, CHIPS, stride=2), :] = jnp.where(first, own, mate)
    rows_ref[pl.ds(1, CHIPS, stride=2), :] = jnp.where(first, mate, own)
    place = jnp.transpose(rows_ref[...])
    far = place[32:64] * place[32:64] + place[64:96] * place[64:96] + place[96:128] * place[96:128]
    distance_ref[...] = jnp.sqrt(far)
    few = lax.broadcasted_iota(jnp.int32, (8, LANES), 0)
    for number in range(32):
        axes = [place[32 * axis + number : 32 * axis + number + 1] for axis in (1, 2, 3)]
        total = jnp.where(few == 0, far[number : number + 1], jnp.where(few == 1, 1.0, 0.0))
        for at, value in enumerate(axes):
            total = jnp.where(few == at + 2, value, total)
        high, mid, low = split3(total)
        zero = jnp.zeros((80, LANES), F32)
        tall = jnp.concatenate([high, high, mid, high, mid, low, zero], axis=0)
        observer_ref[number // 2, :, (number % 2) * LANES : (number % 2 + 1) * LANES] = tall.astype(BF16)


def radiate_kernel(answer_ref, observer_ref, distance_ref, member_ref, info_ref, *refs):
    square_ref, out_ref, panel_ref, push_ref, even_ref, odd_ref, sums_ref = refs
    count = member_ref.shape[1]
    member = member_ref[...]
    spread = [jnp.zeros((LANES, count), F32)] * 2
    for half in range(2):
        for part in split3(answer_ref[pl.ds(half, CHIPS, stride=2), :]):
            spread[half] = spread[half] + lax.dot_general(
                part.astype(BF16), member, (((0,), (0,)), ((), ())), preferred_element_type=F32
            )
    rank = info_ref[16:17]
    weight = info_ref[17:18]
    picked = jnp.zeros((16, count), F32)
    for slot in range(SLOTS):
        lines = spread[slot // 8][slot % 8 * 16 : slot % 8 * 16 + 16]
        picked = picked + jnp.where(rank == slot, lines, 0.0)
    picked = picked * weight
    square = info_ref[0:8]
    offset = info_ref[8:16]
    tall, push = [], []

    def place(number, start, lines):
        at = number * count + start
        panel_ref[at : at + lines.shape[0], :] = lines

    def row(var, which, part):
        at = var * 4 + which * 2 + part
        return picked[at : at + 1]

    for which in range(2):
        wave = info_ref[18 + which : 19 + which]
        flux = [
            wave
            * (
                row(1, which, part) * offset[2:3]
                + row(2, which, part) * offset[3:4]
                + row(3, which, part) * offset[4:5]
            )
            for part in range(2)
        ]
        press = [row(0, which, part) for part in range(2)]
        quantities = [offset * press[0] - square * flux[1], square * flux[0] + offset * press[1]]
        for quantity in quantities:
            high, mid, low = split3(quantity)
            tall += [high, mid, high, low]
        scaled = wave * info_ref[20:21]
        push += [scaled * press[0], scaled * press[1]]
    tall = jnp.concatenate(tall, axis=0)
    low_lanes = lax.broadcasted_iota(jnp.int32, (LANES, LANES), 1) < 32
    push = jnp.concatenate(push + [jnp.zeros((LANES - 4, count), F32)], axis=0)
    for half in range(count // LANES):
        here = slice(half * LANES, (half + 1) * LANES)
        turned = jnp.transpose(tall[:, here])
        for number in range(4):
            shifted = turned if number == 0 else pltpu.roll(turned, LANES - 32 * number, 1)
            place(number, half * LANES, jnp.where(low_lanes, shifted, 0.0).astype(BF16))
        turned = jnp.transpose(push[:, here])
        for number in range(4):
            push_ref[number, here, :] = jnp.broadcast_to(turned[:, number : number + 1], (LANES, LANES))
    for number in range(2):
        place(4 + number, 0, square_ref[number])

    ratio = jnp.broadcast_to(info_ref[21:22, 0:LANES], (8, LANES))

    def project(step, linear_ref):
        views = jnp.concatenate([observer_ref[step * JOIN + at] for at in range(JOIN)], axis=1)
        linear_ref[...] = jnp.dot(panel_ref[...], views, preferred_element_type=F32)

    def tiles(step, now_ref, later_ref):
        for side in range(2 * JOIN):
            lanes = slice(side * LANES, (side + 1) * LANES)
            sums = [jnp.zeros((8, LANES), F32)] * 4
            for first in range(0, count, 8):
                if first % 64 == 0 and side * 4 + first // 64 < 6:
                    number = side * 4 + first // 64
                    lines = pl.ds(number * count, count)
                    following = observer_ref[jnp.minimum(step + 1, TILES // JOIN - 1)]
                    later_ref[lines, :] = jnp.dot(panel_ref[lines, :], following, preferred_element_type=F32)
                rows = slice(first, first + 8)

                def get(number):
                    return now_ref[number * count + first : number * count + first + 8, lanes]

                far = get(4)
                inverse = lax.rsqrt(far)
                distance = far * inverse
                shift = distance * get(5)
                cube = inverse * inverse * inverse
                twice = cube + cube
                for which in range(2):
                    phase = distance * ratio if which else distance
                    phase = phase - jnp.round(phase)
                    z = phase * phase
                    sine = phase * (TAN_TOP[0] + z * TAN_TOP[1])
                    cosine = (z + TAN_LOW[1]) * z + TAN_LOW[0]
                    scale = pl.reciprocal(sine * sine + cosine * cosine, approx=True)
                    part = sine * (scale * twice)
                    sine, cosine = cosine * part, cube - sine * part
                    real = get(2 * which) - shift * push_ref[2 * which + 1, rows, :]
                    imag = get(2 * which + 1) + shift * push_ref[2 * which, rows, :]
                    sums[2 * which] = sums[2 * which] + (cosine * real + sine * imag)
                    sums[2 * which + 1] = sums[2 * which + 1] + (cosine * imag - sine * real)
            for at in range(4):
                line = at * 32 + step * 2 * JOIN + side
                sums_ref[pl.ds(pl.multiple_of(line * 8, 8), 8), :] = sums[at]

    project(0, even_ref)

    def one_step(step, carry):
        pl.when(step % 2 == 0)(lambda: tiles(step, even_ref, odd_ref))
        pl.when(step % 2 == 1)(lambda: tiles(step, odd_ref, even_ref))
        return carry

    lax.fori_loop(0, TILES // JOIN, one_step, 0)
    total = sums_ref[pl.ds(0, LANES, stride=8), :]
    for at in range(1, 8):
        total = total + sums_ref[pl.ds(at, LANES, stride=8), :]
    total = total * jnp.concatenate([distance_ref[...]] * 4, axis=0)
    out_ref[...] = jnp.transpose(total)


def vmem():
    return pl.BlockSpec(memory_space=pltpu.VMEM)


def anywhere():
    return pl.BlockSpec(memory_space=pl.ANY)


def hbm():
    return pl.BlockSpec(memory_space=pltpu.HBM)


def smem():
    return pl.BlockSpec(memory_space=pltpu.SMEM)


ORDER = [(FIRST + at) % CHIPS for at in range(CHIPS)]
SAME_CORE = [[2 * chip + core for chip in ORDER] for core in range(2)]
ALL_CORES = [[2 * chip + core for chip in ORDER for core in range(2)]]


def exchange(value, groups):
    return lax.all_to_all(
        value, "panel", split_axis=0, concat_axis=0, axis_index_groups=groups, tiled=True
    )


def swap(value):
    return lax.ppermute(value, "panel", [(at, at ^ 1) for at in range(2 * CHIPS)])


def local(
    surface,
    fluid_owner,
    cell_row,
    pan_polar,
    pan_azimuth,
    pan_radius,
    pan_area,
    obs_polar,
    obs_azimuth,
    obs_distance,
    harmonic,
):
    per_device = cell_row.shape[0]
    panel_total = per_device * lax.axis_size("panel")
    owner = fluid_owner.reshape(1, per_device)
    table = jax.ShapeDtypeStruct((LANES, LANES), F32)
    params = pltpu.CompilerParams(vmem_limit_bytes=VMEM_LIMIT)
    whole = pltpu.CompilerParams(vmem_limit_bytes=63 * 1024 * 1024)
    line = pltpu.VMEM((1, per_device), F32)
    few = pltpu.VMEM((1, obs_distance.shape[0]), F32)
    names = pltpu.VMEM((1, per_device), jnp.int32)
    ask = pl.pallas_call(
        ask_kernel,
        out_shape=jax.ShapeDtypeStruct((CHIPS, LANES), F32),
        in_specs=[hbm()] * 5,
        out_specs=vmem(),
        scratch_shapes=[names, names, few, few, few, pltpu.SemaphoreType.DMA((5,))],
        compiler_params=whole,
        name="ask",
    )(
        owner,
        cell_row.reshape(1, per_device),
        obs_polar.reshape(1, -1),
        obs_azimuth.reshape(1, -1),
        obs_distance.reshape(1, -1),
    )
    values = pl.pallas_call(
        select_kernel,
        out_shape=jax.ShapeDtypeStruct((8, 2, surface.shape[3]), F32),
        in_specs=[smem(), anywhere(), hbm()],
        out_specs=vmem(),
        scratch_shapes=[pltpu.SemaphoreType.DMA((8,))],
        compiler_params=params,
        cost_estimate=pl.CostEstimate(flops=10**7, bytes_accessed=10**7, transcendentals=0),
        name="select",
    )(harmonic, ask, surface)
    mate_values = swap(values)
    asked = exchange(ask, SAME_CORE)
    found = pl.pallas_call(
        pick_kernel,
        out_shape=table,
        in_specs=[vmem()] * 3,
        out_specs=vmem(),
        scratch_shapes=[pltpu.VMEM((SLOTS * 16, LANES), F32)],
        compiler_params=params,
        name="pick",
    )(asked, values, mate_values)
    answer = exchange(found, SAME_CORE)
    asked, _ = lax.optimization_barrier((asked, found))
    mate_asked = swap(asked)
    member, info, square = pl.pallas_call(
        functools.partial(prepare_kernel, panel_total=panel_total),
        out_shape=(
            jax.ShapeDtypeStruct((CHIPS, per_device), BF16),
            jax.ShapeDtypeStruct((24, per_device), F32),
            jax.ShapeDtypeStruct((2, per_device, LANES), BF16),
        ),
        in_specs=[smem(), anywhere()] + [vmem()] * 5,
        out_specs=(vmem(),) * 3,
        compiler_params=params,
        cost_estimate=pl.CostEstimate(flops=10**7, bytes_accessed=10**7, transcendentals=0),
        name="prepare",
    )(
        harmonic,
        found,
        owner,
        pan_polar.reshape(1, -1),
        pan_azimuth.reshape(1, -1),
        pan_radius.reshape(1, -1),
        pan_area.reshape(1, -1),
    )
    pairs = per_device * 32 * LANES
    observer, distance = pl.pallas_call(
        observers_kernel,
        out_shape=(
            jax.ShapeDtypeStruct((TILES, LANES, 2 * LANES), BF16),
            jax.ShapeDtypeStruct((32, LANES), F32),
        ),
        in_specs=[vmem()] * 2,
        out_specs=(vmem(),) * 2,
        scratch_shapes=[pltpu.VMEM((LANES, LANES), F32)],
        compiler_params=params,
        cost_estimate=pl.CostEstimate(flops=10**7, bytes_accessed=10**7, transcendentals=0),
        name="observers",
    )(asked, mate_asked)
    partial = pl.pallas_call(
        radiate_kernel,
        out_shape=table,
        in_specs=[vmem()] * 6,
        out_specs=vmem(),
        scratch_shapes=[
            pltpu.VMEM((6 * per_device, LANES), BF16),
            pltpu.VMEM((4, per_device, LANES), F32),
            pltpu.VMEM((6 * per_device, 2 * JOIN * LANES), F32),
            pltpu.VMEM((6 * per_device, 2 * JOIN * LANES), F32),
            pltpu.VMEM((8 * LANES, LANES), F32),
        ],
        compiler_params=params,
        cost_estimate=pl.CostEstimate(flops=90 * pairs, bytes_accessed=10**6, transcendentals=3 * pairs),
        name="radiate",
    )(answer, observer, distance, member, info, square)
    partial = exchange(partial, ALL_CORES)
    return jnp.sum(partial, axis=0).reshape(2, 2, obs_distance.shape[0])


def solution(mesh):
    in_specs = (
        P(None, None, None, "panel"),
        P("panel", None),
        P("panel"),
        P("panel"),
        P("panel"),
        P("panel"),
        P("panel"),
        P(("panel", "obs")),
        P(("panel", "obs")),
        P(("panel", "obs")),
        P(),
    )
    out_specs = P(None, None, ("panel", "obs"))
    return jax.shard_map(local, mesh=mesh, in_specs=in_specs, out_specs=out_specs, check_vma=False)
```

```python
import functools
import math

import jax
import jax.numpy as jnp
from jax import lax
from jax.experimental import pallas as pl
from jax.experimental.pallas import tpu as pltpu
from jax.sharding import PartitionSpec as P

BASE_WAVE = 2.0
LANES = 128
CHIPS = 64
FIRST = 40
SLOTS = 16
MAGIC = 12582912.0
F32 = jnp.float32
BF16 = jnp.bfloat16
VMEM_LIMIT = 48 * 1024 * 1024
TILES = 16
JOIN = 1

TAN_TOP = (3.1051745414733887, -2.988323211669922)
TAN_LOW = (0.9884211421012878, -4.203673839569092)


def split3(value):
    high = value.astype(BF16).astype(F32)
    rest = value - high
    mid = rest.astype(BF16).astype(F32)
    return high, mid, rest - mid


def owner_mask(owner):
    rows = lax.broadcasted_iota(jnp.int32, (LANES, owner.shape[1]), 0)
    return jnp.where(rows == owner, 1.0, 0.0).astype(F32)


def rank_of(member):
    count = member.shape[1]
    first = lax.broadcasted_iota(jnp.int32, (count, count), 0)
    second = lax.broadcasted_iota(jnp.int32, (count, count), 1)
    earlier = jnp.where(first < second, 1.0, 0.0).astype(BF16)
    before = jnp.dot(member.astype(BF16), earlier, preferred_element_type=F32)
    return jnp.sum(before * member, axis=0, keepdims=True)


def chip_mask(owner):
    rows = lax.broadcasted_iota(jnp.int32, (CHIPS, owner.shape[1]), 0)
    return jnp.where(rows == ((owner >> 1) + CHIPS - FIRST) % CHIPS, 1.0, 0.0).astype(F32)


def slot_of(owner):
    return rank_of(owner_mask(owner)) + (8 * (owner & 1)).astype(F32)


def fetch(sources, targets, sem):
    copies = [pltpu.make_async_copy(*pair, sem.at[at]) for at, pair in enumerate(zip(sources, targets))]
    for copy in copies:
        copy.start()
    for copy in copies:
        copy.wait()


def ask_kernel(*refs):
    out_ref, owner_ref, cell_ref, polar_ref, azimuth_ref, distance_ref, sem = refs[5:]
    fetch(refs[:5], refs[6:11], sem)
    owner = owner_ref[...]
    place = slot_of(owner)
    cell = cell_ref[...]
    low = (cell & 31).astype(F32)
    high = (cell >> 5).astype(F32)
    slot = lax.broadcasted_iota(jnp.int32, (LANES, cell.shape[1]), 0)
    here = jnp.where((slot & 15).astype(F32) == place, 1.0, 0.0)
    table = here * jnp.where(slot < 16, low, jnp.where(slot < 32, high, 0.0))
    asked = lax.dot_general(
        chip_mask(owner).astype(BF16),
        table.astype(BF16),
        (((1,), (1,)), ((), ())),
        preferred_element_type=F32,
    )
    asked = asked + 32.0 * pltpu.roll(asked, LANES - 16, 1)
    lane = lax.broadcasted_iota(jnp.int32, (CHIPS, LANES), 1)
    polar = polar_ref[...]
    azimuth = azimuth_ref[...]
    distance = distance_ref[...]
    cycle = jnp.sin(polar) * distance
    place = jnp.concatenate(
        [
            jnp.zeros_like(polar),
            cycle * jnp.cos(azimuth),
            cycle * jnp.sin(azimuth),
            distance * jnp.cos(polar),
        ],
        axis=1,
    )
    out_ref[...] = jnp.where(lane < 16, asked, jnp.broadcast_to(place, (CHIPS, LANES)))


def pick_kernel(ask_ref, own_ref, mate_ref, out_ref, rows_ref):
    square = jnp.concatenate([ask_ref[...], jnp.zeros((LANES - CHIPS, LANES), F32)], axis=0)
    wanted = jnp.transpose(square)[0:SLOTS].astype(jnp.int32)
    block = wanted >> 7
    within = wanted & 127
    first = lax.axis_index("panel") % 2 == 0
    own, mate = [
        jnp.concatenate([ref[at] for at in range(8)], axis=0) for ref in (own_ref, mate_ref)
    ]
    values = (jnp.where(first, own, mate), jnp.where(first, mate, own))
    chunks = own.shape[1] // LANES
    for slot in range(SLOTS):
        index = jnp.broadcast_to(within[slot : slot + 1], (16, LANES))
        where = jnp.broadcast_to(block[slot : slot + 1], (16, LANES))
        found = jnp.zeros((16, LANES), F32)
        for chunk in range(chunks):
            part = values[slot // 8][:, chunk * LANES : (chunk + 1) * LANES]
            taken = jnp.take_along_axis(part, index, axis=1)
            found = jnp.where(where == chunk, taken, found)
        rows_ref[slot * 16 : slot * 16 + 16, :] = found
    for half in range(2):
        here = slice(half * LANES, (half + 1) * LANES)
        out_ref[pl.ds(half, CHIPS, stride=2), :] = jnp.transpose(rows_ref[here, :])[0:CHIPS]


def select_kernel(harmonic_ref, after_ref, surface_ref, out_ref, sem):
    sources, targets = [], []
    for var in range(4):
        for which in range(2):
            sources.append(surface_ref.at[var, harmonic_ref[which] - 1])
            targets.append(out_ref.at[2 * var + which])
    fetch(sources, targets, sem)


def prepare_kernel(harmonic_ref, after_ref, *refs, panel_total):
    owner_ref, polar_ref, azimuth_ref, radius_ref, area_ref, member_ref, info_ref, panel_ref = refs
    owner = owner_ref[...]
    count = owner.shape[1]
    member_ref[...] = chip_mask(owner).astype(BF16)
    polar = polar_ref[...]
    azimuth = azimuth_ref[...]
    radius = radius_ref[...]
    cycle = jnp.sin(polar)
    normal = (cycle * jnp.cos(azimuth), cycle * jnp.sin(azimuth), jnp.cos(polar))
    line = lax.broadcasted_iota(jnp.int32, (8, count), 0)

    def stack(*rows):
        total = jnp.zeros((8, count), F32)
        for at, value in enumerate(rows):
            total = jnp.where(line == at, value, total)
        return total

    square = stack(
        jnp.ones_like(radius),
        radius * radius,
        *[-2.0 * radius * axis for axis in normal],
    )
    info_ref[0:8] = square
    info_ref[8:16] = stack(jnp.zeros_like(radius), -radius, *normal)
    weight = area_ref[...] * (0.25 / (math.pi * math.sqrt(panel_total)))
    waves = [BASE_WAVE * harmonic_ref[which].astype(F32) for which in range(2)]
    unit = jnp.full((1, count), waves[0] * (1.0 / (2.0 * math.pi)), F32)
    weight = weight * (unit * unit * unit)
    info_ref[16:24] = stack(slot_of(owner), weight, *waves, 1.0 / unit, waves[1] * ((1.0 / (2.0 * math.pi)) / unit))

    zero = jnp.zeros((80, count), F32)
    for at, quantity in enumerate((square * (unit * unit), info_ref[8:16])):
        high, mid, low = split3(quantity)
        tall = jnp.concatenate([high, mid, high, low, mid, high, zero], axis=0)
        for half in range(count // LANES):
            panel_ref[at, half * LANES : (half + 1) * LANES, :] = jnp.transpose(
                tall[:, half * LANES : (half + 1) * LANES]
            ).astype(BF16)


def observers_kernel(own_ref, mate_ref, observer_ref, distance_ref, rows_ref):
    first = lax.axis_index("panel") % 2 == 0
    own, mate = own_ref[...], mate_ref[...]
    rows_ref[pl.ds(0, CHIPS, stride=2), :] = jnp.where(first, own, mate)
    rows_ref[pl.ds(1, CHIPS, stride=2), :] = jnp.where(first, mate, own)
    place = jnp.transpose(rows_ref[...])
    far = place[32:64] * place[32:64] + place[64:96] * place[64:96] + place[96:128] * place[96:128]
    distance_ref[...] = jnp.sqrt(far)
    few = lax.broadcasted_iota(jnp.int32, (8, LANES), 0)
    for number in range(32):
        axes = [place[32 * axis + number : 32 * axis + number + 1] for axis in (1, 2, 3)]
        total = jnp.where(few == 0, far[number : number + 1], jnp.where(few == 1, 1.0, 0.0))
        for at, value in enumerate(axes):
            total = jnp.where(few == at + 2, value, total)
        high, mid, low = split3(total)
        zero = jnp.zeros((80, LANES), F32)
        tall = jnp.concatenate([high, high, mid, high, mid, low, zero], axis=0)
        observer_ref[number // 2, :, (number % 2) * LANES : (number % 2 + 1) * LANES] = tall.astype(BF16)


def radiate_kernel(answer_ref, observer_ref, distance_ref, member_ref, info_ref, *refs):
    square_ref, out_ref, panel_ref, push_ref, even_ref, odd_ref, sums_ref = refs
    count = member_ref.shape[1]
    member = member_ref[...]
    spread = [jnp.zeros((LANES, count), F32)] * 2
    for half in range(2):
        for part in split3(answer_ref[pl.ds(half, CHIPS, stride=2), :]):
            spread[half] = spread[half] + lax.dot_general(
                part.astype(BF16), member, (((0,), (0,)), ((), ())), preferred_element_type=F32
            )
    rank = info_ref[16:17]
    weight = info_ref[17:18]
    picked = jnp.zeros((16, count), F32)
    for slot in range(SLOTS):
        lines = spread[slot // 8][slot % 8 * 16 : slot % 8 * 16 + 16]
        picked = picked + jnp.where(rank == slot, lines, 0.0)
    picked = picked * weight
    square = info_ref[0:8]
    offset = info_ref[8:16]
    tall, push = [], []

    def place(number, start, lines):
        at = number * count + start
        panel_ref[at : at + lines.shape[0], :] = lines

    def row(var, which, part):
        at = var * 4 + which * 2 + part
        return picked[at : at + 1]

    for which in range(2):
        wave = info_ref[18 + which : 19 + which]
        flux = [
            wave
            * (
                row(1, which, part) * offset[2:3]
                + row(2, which, part) * offset[3:4]
                + row(3, which, part) * offset[4:5]
            )
            for part in range(2)
        ]
        press = [row(0, which, part) for part in range(2)]
        quantities = [offset * press[0] - square * flux[1], square * flux[0] + offset * press[1]]
        for quantity in quantities:
            high, mid, low = split3(quantity)
            tall += [high, mid, high, low]
        scaled = wave * info_ref[20:21]
        push += [scaled * press[0], scaled * press[1]]
    tall = jnp.concatenate(tall, axis=0)
    low_lanes = lax.broadcasted_iota(jnp.int32, (LANES, LANES), 1) < 32
    push = jnp.concatenate(push + [jnp.zeros((LANES - 4, count), F32)], axis=0)
    for half in range(count // LANES):
        here = slice(half * LANES, (half + 1) * LANES)
        turned = jnp.transpose(tall[:, here])
        for number in range(4):
            shifted = turned if number == 0 else pltpu.roll(turned, LANES - 32 * number, 1)
            place(number, half * LANES, jnp.where(low_lanes, shifted, 0.0).astype(BF16))
        turned = jnp.transpose(push[:, here])
        for number in range(4):
            push_ref[number, here, :] = jnp.broadcast_to(turned[:, number : number + 1], (LANES, LANES))
    for number in range(2):
        place(4 + number, 0, square_ref[number])

    ratio = jnp.broadcast_to(info_ref[21:22, 0:LANES], (8, LANES))

    def project(step, linear_ref):
        views = jnp.concatenate([observer_ref[step * JOIN + at] for at in range(JOIN)], axis=1)
        linear_ref[...] = jnp.dot(panel_ref[...], views, preferred_element_type=F32)

    def tiles(step, now_ref, later_ref):
        for side in range(2 * JOIN):
            lanes = slice(side * LANES, (side + 1) * LANES)
            sums = [jnp.zeros((8, LANES), F32)] * 4
            for first in range(0, count, 8):
                if first % 64 == 0 and side * 4 + first // 64 < 6:
                    number = side * 4 + first // 64
                    lines = pl.ds(number * count, count)
                    following = observer_ref[jnp.minimum(step + 1, TILES // JOIN - 1)]
                    later_ref[lines, :] = jnp.dot(panel_ref[lines, :], following, preferred_element_type=F32)
                rows = slice(first, first + 8)

                def get(number):
                    return now_ref[number * count + first : number * count + first + 8, lanes]

                far = get(4)
                inverse = lax.rsqrt(far)
                distance = far * inverse
                shift = distance * get(5)
                cube = inverse * inverse * inverse
                twice = cube + cube
                for which in range(2):
                    phase = distance * ratio if which else distance
                    phase = phase - jnp.round(phase)
                    z = phase * phase
                    sine = phase * (TAN_TOP[0] + z * TAN_TOP[1])
                    cosine = (z + TAN_LOW[1]) * z + TAN_LOW[0]
                    scale = pl.reciprocal(sine * sine + cosine * cosine, approx=True)
                    part = sine * (scale * twice)
                    sine, cosine = cosine * part, cube - sine * part
                    real = get(2 * which) - shift * push_ref[2 * which + 1, rows, :]
                    imag = get(2 * which + 1) + shift * push_ref[2 * which, rows, :]
                    sums[2 * which] = sums[2 * which] + (cosine * real + sine * imag)
                    sums[2 * which + 1] = sums[2 * which + 1] + (cosine * imag - sine * real)
            for at in range(4):
                line = at * 32 + step * 2 * JOIN + side
                sums_ref[pl.ds(pl.multiple_of(line * 8, 8), 8), :] = sums[at]

    project(0, even_ref)

    def one_step(step, carry):
        pl.when(step % 2 == 0)(lambda: tiles(step, even_ref, odd_ref))
        pl.when(step % 2 == 1)(lambda: tiles(step, odd_ref, even_ref))
        return carry

    lax.fori_loop(0, TILES // JOIN, one_step, 0)
    total = sums_ref[pl.ds(0, LANES, stride=8), :]
    for at in range(1, 8):
        total = total + sums_ref[pl.ds(at, LANES, stride=8), :]
    total = total * jnp.concatenate([distance_ref[...]] * 4, axis=0)
    out_ref[...] = jnp.transpose(total)


def finish_kernel(part_ref, out_ref):
    line = jnp.sum(part_ref[...], axis=0, keepdims=True)
    width = out_ref.shape[2]
    for which in range(2):
        for part in range(2):
            at = (2 * which + part) * width
            out_ref[which, part : part + 1, :] = line[:, at : at + width]


def vmem():
    return pl.BlockSpec(memory_space=pltpu.VMEM)


def anywhere():
    return pl.BlockSpec(memory_space=pl.ANY)


def hbm():
    return pl.BlockSpec(memory_space=pltpu.HBM)


def smem():
    return pl.BlockSpec(memory_space=pltpu.SMEM)


ORDER = [(FIRST + at) % CHIPS for at in range(CHIPS)]
SAME_CORE = [[2 * chip + core for chip in ORDER] for core in range(2)]
ALL_CORES = [[2 * chip + core for chip in ORDER for core in range(2)]]


def exchange(value, groups):
    return lax.all_to_all(
        value, "panel", split_axis=0, concat_axis=0, axis_index_groups=groups, tiled=True
    )


def swap(value):
    return lax.ppermute(value, "panel", [(at, at ^ 1) for at in range(2 * CHIPS)])


def local(
    surface,
    fluid_owner,
    cell_row,
    pan_polar,
    pan_azimuth,
    pan_radius,
    pan_area,
    obs_polar,
    obs_azimuth,
    obs_distance,
    harmonic,
):
    per_device = cell_row.shape[0]
    panel_total = per_device * lax.axis_size("panel")
    owner = fluid_owner.reshape(1, per_device)
    table = jax.ShapeDtypeStruct((LANES, LANES), F32)
    params = pltpu.CompilerParams(vmem_limit_bytes=VMEM_LIMIT)
    whole = pltpu.CompilerParams(vmem_limit_bytes=63 * 1024 * 1024)
    line = pltpu.VMEM((1, per_device), F32)
    few = pltpu.VMEM((1, obs_distance.shape[0]), F32)
    names = pltpu.VMEM((1, per_device), jnp.int32)
    ask = pl.pallas_call(
        ask_kernel,
        out_shape=jax.ShapeDtypeStruct((CHIPS, LANES), F32),
        in_specs=[hbm()] * 5,
        out_specs=vmem(),
        scratch_shapes=[names, names, few, few, few, pltpu.SemaphoreType.DMA((5,))],
        compiler_params=whole,
        name="ask",
    )(
        owner,
        cell_row.reshape(1, per_device),
        obs_polar.reshape(1, -1),
        obs_azimuth.reshape(1, -1),
        obs_distance.reshape(1, -1),
    )
    values = pl.pallas_call(
        select_kernel,
        out_shape=jax.ShapeDtypeStruct((8, 2, surface.shape[3]), F32),
        in_specs=[smem(), anywhere(), hbm()],
        out_specs=vmem(),
        scratch_shapes=[pltpu.SemaphoreType.DMA((8,))],
        compiler_params=params,
        cost_estimate=pl.CostEstimate(flops=10**7, bytes_accessed=10**7, transcendentals=0),
        name="select",
    )(harmonic, ask, surface)
    mate_values = swap(values)
    asked = exchange(ask, SAME_CORE)
    found = pl.pallas_call(
        pick_kernel,
        out_shape=table,
        in_specs=[vmem()] * 3,
        out_specs=vmem(),
        scratch_shapes=[pltpu.VMEM((SLOTS * 16, LANES), F32)],
        compiler_params=params,
        name="pick",
    )(asked, values, mate_values)
    answer = exchange(found, SAME_CORE)
    asked, _ = lax.optimization_barrier((asked, found))
    mate_asked = swap(asked)
    member, info, square = pl.pallas_call(
        functools.partial(prepare_kernel, panel_total=panel_total),
        out_shape=(
            jax.ShapeDtypeStruct((CHIPS, per_device), BF16),
            jax.ShapeDtypeStruct((24, per_device), F32),
            jax.ShapeDtypeStruct((2, per_device, LANES), BF16),
        ),
        in_specs=[smem(), anywhere()] + [vmem()] * 5,
        out_specs=(vmem(),) * 3,
        compiler_params=params,
        cost_estimate=pl.CostEstimate(flops=10**7, bytes_accessed=10**7, transcendentals=0),
        name="prepare",
    )(
        harmonic,
        found,
        owner,
        pan_polar.reshape(1, -1),
        pan_azimuth.reshape(1, -1),
        pan_radius.reshape(1, -1),
        pan_area.reshape(1, -1),
    )
    pairs = per_device * 32 * LANES
    observer, distance = pl.pallas_call(
        observers_kernel,
        out_shape=(
            jax.ShapeDtypeStruct((TILES, LANES, 2 * LANES), BF16),
            jax.ShapeDtypeStruct((32, LANES), F32),
        ),
        in_specs=[vmem()] * 2,
        out_specs=(vmem(),) * 2,
        scratch_shapes=[pltpu.VMEM((LANES, LANES), F32)],
        compiler_params=params,
        cost_estimate=pl.CostEstimate(flops=10**7, bytes_accessed=10**7, transcendentals=0),
        name="observers",
    )(asked, mate_asked)
    partial = pl.pallas_call(
        radiate_kernel,
        out_shape=table,
        in_specs=[vmem()] * 6,
        out_specs=vmem(),
        scratch_shapes=[
            pltpu.VMEM((6 * per_device, LANES), BF16),
            pltpu.VMEM((4, per_device, LANES), F32),
            pltpu.VMEM((6 * per_device, 2 * JOIN * LANES), F32),
            pltpu.VMEM((6 * per_device, 2 * JOIN * LANES), F32),
            pltpu.VMEM((8 * LANES, LANES), F32),
        ],
        compiler_params=params,
        cost_estimate=pl.CostEstimate(flops=90 * pairs, bytes_accessed=10**6, transcendentals=3 * pairs),
        name="radiate",
    )(answer, observer, distance, member, info, square)
    partial = exchange(partial, ALL_CORES)
    return pl.pallas_call(
        finish_kernel,
        out_shape=jax.ShapeDtypeStruct((2, 2, obs_distance.shape[0]), F32),
        in_specs=[vmem()],
        out_specs=vmem(),
        compiler_params=params,
        name="finish",
    )(partial)


def solution(mesh):
    in_specs = (
        P(None, None, None, "panel"),
        P("panel", None),
        P("panel"),
        P("panel"),
        P("panel"),
        P("panel"),
        P("panel"),
        P(("panel", "obs")),
        P(("panel", "obs")),
        P(("panel", "obs")),
        P(),
    )
    out_specs = P(None, None, ("panel", "obs"))
    return jax.shard_map(local, mesh=mesh, in_specs=in_specs, out_specs=out_specs, check_vma=False)
```
